32 devices in a mesh: pulse: 8 (over z, y), rng: 4 (over x, core).
Axes of the slice: x: 2, y: 2, z: 4, core: 2. Of those that a mesh axis runs over, the one named last changes fastest.
Arguments:
- echoes: bfloat16 [2, 1024, 8192], P(None, 'pulse', 'rng'), may hold values from -6 to 6
- range_ref: bfloat16 [2, 1024], replicated, may hold values from -0.125 to 0.125
- band_weights: bfloat16 [64, 8192], P(None, 'rng'), may hold values from -0.75 to 0.75
- band_offsets: int32 [8192], P('rng'), may hold values from 0 to 32, as said below
- azimuth_ref: bfloat16 [2, 512], replicated, may hold values from -0.1875 to 0.1875
Outputs:
- image: float32 [2, 4, 2048, 1024], P(None, 'rng', 'pulse')
The draws below stay inside these ranges and needn't reach their ends.
Inputs may be any that keep to these rules, and one draw needn't show every extreme that they name: `band_offsets`: every value from 0 to one half of 64 may occur; both ends occur in every draw.
All inputs are finite; a program needn't handle non-finite values.
Results may differ from the reference program's by a relative error of at most 0.0041.
Values may be sent and summed in bfloat16 or wider, within the bound.
No kernel may reach another device: no remote copies, remote signals or barrier semaphores. Data moves between devices by JAX's collectives and lax.ppermute only.
A program may use at most 64 MiB of HBM per device.

```python
import math
from functools import partial
import jax
import jax.numpy as jnp
from jax import lax

R = 8192
RT = 1024
AT = 512
BAND = 64
BLK = 128
PULSES = 1024
N_RNG = 4


def draw_band_offsets(key, part):
    key_values, key_high, key_low = jax.random.split(jax.random.fold_in(key, 17), 3)
    values = jax.random.randint(key_values, (R,), 0, BAND // 2 + 1)
    high_spot = jax.random.randint(key_high, (), 0, R)
    low_spot = jax.random.randint(key_low, (), 0, R)
    positions = jnp.arange(R)
    values = jnp.where(positions == high_spot, BAND // 2, values)
    values = jnp.where((positions == low_spot) & (positions != high_spot), 0, values)
    return values.astype(jnp.int32)


def block_scale(key, dims, cuts, low, high):
    def one(dim, parts):
        steps = jax.random.uniform(jax.random.fold_in(jax.random.fold_in(key, 6), dim), (parts,), jnp.float32, low / len(cuts), high / len(cuts))
        return jnp.repeat(jnp.exp(steps), dims[dim] // parts).reshape((-1,) + (1,) * (len(dims) - dim - 1))

    factor_of = one(*cuts[0])
    for cut in cuts[1:]:
        factor_of = factor_of * one(*cut)
    return factor_of


def centred(key, dims, spread, limit, pieces=(), held_as=jnp.bfloat16):
    entries = spread * jax.random.normal(key, dims, jnp.float32)
    if pieces:
        entries = entries * block_scale(key, dims, pieces, -0.22, 0.18)
    return jnp.clip(entries, -limit, limit).astype(held_as)


def setup_inputs(seed: int = 0) -> dict:
    arg_keys = jax.random.split(jax.random.key(seed), 6)
    return {
        "echoes": centred(arg_keys[0], (2, PULSES, R), 1.0, 6.0, ((1, 8), (2, 4))),
        "range_ref": centred(arg_keys[1], (2, RT), (2 * RT) ** -0.5, 0.125),
        "band_weights": centred(arg_keys[2], (BAND, R), BAND ** -0.5, 0.75, ((1, 4),)),
        "band_offsets": draw_band_offsets(jax.random.fold_in(arg_keys[5], 71), 0),
        "azimuth_ref": centred(arg_keys[4], (2, AT), (2 * AT) ** -0.5, 0.1875),
    }


def toeplitz_real(filter_taps, block_count):
    tap_total = filter_taps.shape[1]
    in_index = jnp.arange(BLK, dtype=jnp.int32)[:, None]
    out_index = jnp.arange(BLK, dtype=jnp.int32)[None, :]
    tap_index = (jnp.arange(block_count, dtype=jnp.int32) * BLK)[:, None, None] + in_index - out_index
    usable = (tap_index >= 0) & (tap_index < tap_total)
    clipped = jnp.clip(tap_index, 0, tap_total - 1)
    zero_tap = jnp.zeros((), filter_taps.dtype)
    real_part = jnp.where(usable, filter_taps[0][clipped], zero_tap)
    imag_part = jnp.where(usable, filter_taps[1][clipped], zero_tap)
    upper = jnp.stack([real_part, -imag_part], axis=2)
    lower = jnp.stack([imag_part, real_part], axis=2)
    return jnp.stack([upper, lower], axis=1)


def correlate_ref(blocks, kernel, out_blocks):
    running = None
    for tap_block in range(kernel.shape[0]):
        window = blocks[:, :, tap_block:tap_block + out_blocks].astype(jnp.float32)
        partial_sum = jnp.einsum("zrbi,ziwc->wrbc", window, kernel[tap_block].astype(jnp.float32), precision=lax.Precision.HIGHEST)
        running = partial_sum if running is None else running + partial_sum
    return running


def grouped_correlate(blocks, kernel, out_blocks):
    row_total = blocks.shape[1]
    group_size = math.gcd(row_total, 256)
    stacked = blocks.reshape(2, row_total // group_size, group_size, blocks.shape[2], BLK).transpose(1, 0, 2, 3, 4)
    outputs = lax.map(partial(correlate_ref, kernel=kernel, out_blocks=out_blocks), stacked)
    return outputs.transpose(1, 0, 2, 3, 4).reshape(2, row_total, out_blocks, BLK)


def band_matrices(weights_t, offsets, block_total):
    table = weights_t.reshape(BAND, block_total, BLK).transpose(1, 0, 2)
    shifts = offsets.reshape(block_total, 1, BLK).astype(jnp.int32)
    in_index = jnp.arange(2 * BLK, dtype=jnp.int32)[None, :, None]
    out_index = jnp.arange(BLK, dtype=jnp.int32)[None, None, :]
    tap_index = in_index - out_index - shifts - BAND // 2
    usable = (tap_index >= 0) & (tap_index < BAND)
    picked = jnp.take_along_axis(table, jnp.clip(tap_index, 0, BAND - 1), axis=1)
    return jnp.where(usable, picked, jnp.zeros((), table.dtype))


def migrate_padded(padded, weights_t, offsets):
    block_total = offsets.shape[0] // BLK
    matrices = band_matrices(weights_t, offsets, block_total).astype(jnp.float32)
    pulse_total = padded.shape[1]
    tiles = padded.reshape(2, pulse_total, block_total + 1, BLK).astype(jnp.float32)
    lower = jnp.einsum("zrbi,bic->zbcr", tiles[:, :, :-1], matrices[:, :BLK], precision=lax.Precision.HIGHEST)
    upper = jnp.einsum("zrbi,bic->zbcr", tiles[:, :, 1:], matrices[:, BLK:], precision=lax.Precision.HIGHEST)
    return (lower + upper).reshape(2, block_total * BLK, pulse_total).astype(jnp.bfloat16)


def azimuth_focus(migrated, kernel):
    bin_total = migrated.shape[1]
    pulse_total = migrated.shape[2]
    padded = jnp.pad(migrated, ((0, 0), (0, 0), (AT // 2, AT // 2)))
    blocks = padded.reshape(2, bin_total, (pulse_total + AT) // BLK, BLK)
    return grouped_correlate(blocks, kernel, pulse_total // BLK).reshape(2, bin_total, pulse_total)


def reference(echoes, range_ref, band_weights, band_offsets, azimuth_ref):
    pulse_total = echoes.shape[1]
    range_kernel = toeplitz_real(range_ref, RT // BLK + 1)
    extended = jnp.pad(echoes, ((0, 0), (0, 0), (0, RT)))
    blocks = extended.reshape(2, pulse_total, (R + RT) // BLK, BLK)
    compressed = grouped_correlate(blocks, range_kernel, R // BLK).reshape(2, pulse_total, R).astype(jnp.bfloat16)
    padded = jnp.pad(compressed, ((0, 0), (0, 0), (BAND, BAND)))
    migrated = migrate_padded(padded, band_weights, band_offsets)
    focused = azimuth_focus(migrated, toeplitz_real(azimuth_ref, AT // BLK + 1))
    return focused.reshape(2, N_RNG, R // N_RNG, pulse_total)
```

```python
import functools

import jax
import jax.numpy as jnp
from jax import lax
from jax.experimental import pallas as pl
from jax.experimental.pallas import tpu as pltpu
from jax.sharding import PartitionSpec as P

RT = 1024
AT = 512
BAND = 64
BLK = 128
HALF = BLK // 2
WIDE = 2 * BLK
RANGE_TILES = RT // BLK + 2
AZ_TILES = AT // BLK + 1
HEAD = RT // BLK + 1
GROUP = 2 * BLK
LIMIT = 24 * 1024 * 1024

VMEM = functools.partial(pl.BlockSpec, memory_space=pltpu.VMEM)
SMEM = functools.partial(pl.BlockSpec, memory_space=pltpu.SMEM)


def params():
    return pltpu.CompilerParams(vmem_limit_bytes=LIMIT)


def pack_head_body(echoes, head, last):
    for block in range(HEAD):
        for part in range(2):
            head[block, :, part * BLK : (part + 1) * BLK] = echoes[
                part, :, block * BLK : (block + 1) * BLK
            ]
    for part in range(2):
        last[0, :, part * BLK : (part + 1) * BLK] = echoes[part, :, -BLK:]


def pack_head(echoes):
    pulses = echoes.shape[1]
    return pl.pallas_call(
        pack_head_body,
        out_shape=(
            jax.ShapeDtypeStruct((HEAD, pulses, WIDE), jnp.bfloat16),
            jax.ShapeDtypeStruct((1, pulses, WIDE), jnp.bfloat16),
        ),
        in_specs=[VMEM()],
        out_specs=(VMEM(), VMEM()),
        compiler_params=params(),
        name="pack_head",
    )(echoes)


def toeplitz_tiles(taps, tiles, out):
    skewed = []
    for part in range(2):
        row = jnp.broadcast_to(taps[part : part + 1, :].astype(jnp.float32), (BLK, taps.shape[1]))
        skewed.append(pltpu.roll(row, 0, 1, stride=1, stride_axis=0))
    for tile in range(tiles):
        span = slice((tile + 1) * BLK, (tile + 2) * BLK)
        real = skewed[0][:, span].T
        imag = skewed[1][:, span].T
        out[tile, :BLK, :BLK] = real.astype(jnp.bfloat16)
        out[tile, :BLK, BLK:] = (-imag).astype(jnp.bfloat16)
        out[tile, BLK:, :BLK] = imag.astype(jnp.bfloat16)
        out[tile, BLK:, BLK:] = real.astype(jnp.bfloat16)


def prepare_body(first, range_taps, az_taps, weights, offsets, range_out, az_out, band_out):
    toeplitz_tiles(range_taps, RANGE_TILES, range_out)
    toeplitz_tiles(az_taps, AZ_TILES, az_out)
    bins = weights.shape[1]
    lane = lax.broadcasted_iota(jnp.int32, (BLK, WIDE), 1)
    for block in range(bins // BLK):
        span = slice(block * BLK, (block + 1) * BLK)
        placed = jnp.concatenate(
            [weights[:, span].astype(jnp.float32), jnp.zeros((BLK - BAND, BLK), jnp.float32)], axis=0
        )
        shifts = offsets[:, span]
        for bit in range((BAND // 2).bit_length()):
            chosen = jnp.broadcast_to((shifts >> bit) & 1, (BLK, BLK)) == 1
            placed = jnp.where(chosen, pltpu.roll(placed, 1 << bit, 0), placed)
        wide = jnp.concatenate([placed.T, jnp.zeros((BLK, BLK), jnp.float32)], axis=1)
        skewed = pltpu.roll(wide, BAND // 2, 1, stride=1, stride_axis=0)
        if block == 0:
            skewed = jnp.where((first[0] == 1) & (lane < HALF), 0.0, skewed)
        band_out[span, :] = skewed.astype(jnp.bfloat16)


def prepare(first, range_ref, azimuth_ref, weights, offsets):
    bins = weights.shape[1]
    range_taps = jnp.pad(range_ref, ((0, 0), (BLK + HALF, BLK + HALF)))
    az_taps = jnp.pad(azimuth_ref, ((0, 0), (BLK, BLK)))
    return pl.pallas_call(
        prepare_body,
        out_shape=(
            jax.ShapeDtypeStruct((RANGE_TILES, WIDE, WIDE), jnp.bfloat16),
            jax.ShapeDtypeStruct((AZ_TILES, WIDE, WIDE), jnp.bfloat16),
            jax.ShapeDtypeStruct((bins, WIDE), jnp.bfloat16),
        ),
        in_specs=[SMEM()] + [VMEM()] * 4,
        out_specs=(VMEM(),) * 3,
        compiler_params=params(),
        name="prepare",
    )(first, range_taps, az_taps, weights, offsets.reshape(1, bins))


def assemble_body(left, head, echoes, right, out):
    out[0] = left[0]
    out[1 : HEAD + 1] = head[...]
    blocks = echoes.shape[2] // BLK
    for block in range(HEAD, blocks):
        for part in range(2):
            out[block + 1, :, part * BLK : (part + 1) * BLK] = echoes[
                part, :, block * BLK : (block + 1) * BLK
            ]
    out[blocks + 1 :] = right[...]


def assemble(left, head, echoes, right):
    pulses = echoes.shape[1]
    blocks = 1 + echoes.shape[2] // BLK + HEAD
    return pl.pallas_call(
        assemble_body,
        out_shape=jax.ShapeDtypeStruct((blocks, pulses, WIDE), jnp.bfloat16),
        in_specs=[VMEM()] * 4,
        out_specs=VMEM(),
        compiler_params=params(),
        name="assemble",
    )(left, head, echoes, right)


def focus_range_body(which, samples, range_tiles, bands, *outs):
    pulses = samples.shape[1]
    for place, out in enumerate(outs):
        group = which[place]
        total = jnp.zeros((3 * pulses, WIDE), jnp.float32)
        for tile in range(RANGE_TILES):
            window = samples[pl.ds(2 * group + tile, 3)].reshape(3 * pulses, WIDE)
            total += jnp.dot(window, range_tiles[tile], preferred_element_type=jnp.float32)
        compressed = total.astype(jnp.bfloat16)
        for half in range(2):
            low = compressed[half * pulses : (half + 1) * pulses]
            high = compressed[(half + 1) * pulses : (half + 2) * pulses]
            reach = jnp.concatenate(
                [
                    jnp.concatenate([low[:, :BLK], high[:, :BLK]], axis=1),
                    jnp.concatenate([low[:, BLK:], high[:, BLK:]], axis=1),
                ],
                axis=0,
            )
            start = pl.multiple_of(group * GROUP + half * BLK, BLK)
            migrated = lax.dot_general(
                bands[pl.ds(start, BLK)],
                reach,
                (((1,), (1,)), ((), ())),
                preferred_element_type=jnp.float32,
            )
            out[half * BLK : (half + 1) * BLK, :] = migrated.astype(jnp.bfloat16)


def focus_range(groups, samples, range_tiles, bands):
    pulses = samples.shape[1]
    count = len(groups)
    return pl.pallas_call(
        focus_range_body,
        out_shape=(jax.ShapeDtypeStruct((GROUP, 2 * pulses), jnp.bfloat16),) * count,
        in_specs=[SMEM()] + [VMEM()] * 3,
        out_specs=(VMEM(),) * count,
        compiler_params=params(),
        name="focus_range",
    )(jnp.stack(groups).astype(jnp.int32), samples, range_tiles, bands)


def focus_azimuth_body(where, az_tiles, *rest):
    parts, out, rows = rest[:-2], rest[-2], rest[-1]
    count = len(parts)
    bins = parts[0].shape[0]
    edge = (AZ_TILES // 2) * bins
    rows[:edge] = jnp.zeros((edge, WIDE), jnp.bfloat16)
    rows[edge + count * bins :] = jnp.zeros((edge, WIDE), jnp.bfloat16)
    for place, part in enumerate(parts):
        start = pl.multiple_of(edge + where[place] * bins, bins)
        rows[pl.ds(start, bins)] = part[...]
    for block in range(count):
        total = jnp.zeros((bins, WIDE), jnp.float32)
        for tile in range(AZ_TILES):
            if 0 <= block + tile - AZ_TILES // 2 < count:
                total += jnp.dot(
                    rows[(block + tile) * bins : (block + tile + 1) * bins],
                    az_tiles[tile],
                    preferred_element_type=jnp.float32,
                )
        for part in range(2):
            out[part, 0, :, block * BLK : (block + 1) * BLK] = total[
                :, part * BLK : (part + 1) * BLK
            ]


def focus_azimuth(where, az_tiles, parts):
    count = len(parts)
    bins = parts[0].shape[0]
    return pl.pallas_call(
        focus_azimuth_body,
        out_shape=jax.ShapeDtypeStruct((2, 1, bins, count * BLK), jnp.float32),
        in_specs=[SMEM()] + [VMEM()] * (1 + count),
        out_specs=VMEM(),
        scratch_shapes=[pltpu.VMEM(((count + AZ_TILES - 1) * bins, WIDE), jnp.bfloat16)],
        compiler_params=params(),
        name="focus_azimuth",
    )(jnp.stack(where).astype(jnp.int32), az_tiles, *parts)


def per_device(echoes, range_ref, band_weights, band_offsets, azimuth_ref):
    quarter_len = echoes.shape[2]
    peers = lax.axis_size("pulse")
    quarters = lax.axis_size("rng")
    bins = quarter_len // peers
    me = lax.axis_index("pulse")
    down = [(i + 1, i) for i in range(quarters - 1)]
    up = [(i, i + 1) for i in range(quarters - 1)]

    head, last = pack_head(echoes)
    right = lax.ppermute(head, "rng", down)
    left = lax.ppermute(last, "rng", up)
    first = (lax.axis_index("rng") == 0).astype(jnp.int32).reshape(1)
    head, band_offsets = lax.optimization_barrier((head, band_offsets))
    range_tiles, az_tiles, bands = prepare(
        first, range_ref, azimuth_ref, band_weights, band_offsets
    )
    samples = assemble(left, head, echoes, right)

    if bins == GROUP and peers & (peers - 1) == 0:
        order = list(range(peers // 2, peers)) + list(range(1, peers // 2)) + [0]
        steps = [order[:1], order[1 : peers // 2], order[peers // 2 :]]
        parts, where = [], []
        for step in steps:
            groups = [me ^ k for k in step]
            made = focus_range(groups, samples, range_tiles, bands)
            for k, piece in zip(step, made):
                if k:
                    parts.append(lax.ppermute(piece, "pulse", [(i, i ^ k) for i in range(peers)]))
                else:
                    parts.append(piece)
                where.append(me ^ k)
            samples, made = lax.optimization_barrier((samples, made))
    else:
        made = focus_range(
            [jnp.int32(g) for g in range(quarter_len // GROUP)], samples, range_tiles, bands
        )
        migrated = jnp.concatenate(made, axis=0)
        swapped = lax.all_to_all(
            migrated.reshape(peers, bins, WIDE), "pulse", split_axis=0, concat_axis=0, tiled=True
        )
        parts = [swapped[i] for i in range(peers)]
        where = [jnp.int32(i) for i in range(peers)]
    return focus_azimuth(where, az_tiles, parts)


def solution(mesh):
    return jax.shard_map(
        per_device,
        mesh=mesh,
        in_specs=(P(None, "pulse", "rng"), P(), P(None, "rng"), P("rng"), P()),
        out_specs=P(None, "rng", "pulse", None),
        check_vma=False,
    )
```

```python
import functools

import jax
import jax.numpy as jnp
from jax import lax
from jax.experimental import pallas as pl
from jax.experimental.pallas import tpu as pltpu
from jax.sharding import PartitionSpec as P

RT = 1024
AT = 512
BAND = 64
BLK = 128
HALF = BLK // 2
WIDE = 2 * BLK
RANGE_TILES = RT // BLK + 2
AZ_TILES = AT // BLK + 1
HEAD = RT // BLK + 1
GROUP = 2 * BLK
LIMIT = 24 * 1024 * 1024

VMEM = functools.partial(pl.BlockSpec, memory_space=pltpu.VMEM)
SMEM = functools.partial(pl.BlockSpec, memory_space=pltpu.SMEM)
HBM = functools.partial(pl.BlockSpec, memory_space=pltpu.HBM)


def call(body, name, out_shape, in_specs, out_specs, scratch_shapes=()):
    return pl.pallas_call(
        body,
        out_shape=out_shape,
        in_specs=in_specs,
        out_specs=out_specs,
        scratch_shapes=scratch_shapes,
        compiler_params=pltpu.CompilerParams(vmem_limit_bytes=LIMIT),
        cost_estimate=pl.CostEstimate(flops=0, bytes_accessed=0, transcendentals=0),
        name=name,
    )


def bf16(*shape):
    return jax.ShapeDtypeStruct(shape, jnp.bfloat16)


def pack_body(place, echoes, near, far):
    odd = place[0] % 2 == 1

    def fill(down, up):
        for part in range(2):
            lanes = slice(part * BLK, (part + 1) * BLK)
            for block in range(HEAD):
                down[block, :, lanes] = echoes[part, :, block * BLK : (block + 1) * BLK]
            up[0, :, lanes] = echoes[part, :, echoes.shape[2] - BLK :]

    pl.when(odd)(lambda: fill(near, far))
    pl.when(jnp.logical_not(odd))(lambda: fill(far, near))


def pack(place, echoes):
    return call(
        pack_body,
        "pack",
        (bf16(HEAD, echoes.shape[1], WIDE),) * 2,
        [SMEM(), VMEM()],
        (VMEM(),) * 2,
    )(place, echoes)


def toeplitz_tiles(taps, tiles, shift, out):
    width = (tiles + 1) * BLK
    skewed = []
    for part in range(2):
        row = jnp.concatenate(
            [
                jnp.zeros((1, BLK), jnp.float32),
                taps[part : part + 1, :].astype(jnp.float32),
                jnp.zeros((1, width - BLK - taps.shape[1]), jnp.float32),
            ],
            axis=1,
        )
        row = jnp.broadcast_to(row, (BLK, width))
        skewed.append(pltpu.roll(row, shift, 1, stride=1, stride_axis=0))
    for tile in range(tiles):
        span = slice((tile + 1) * BLK, (tile + 2) * BLK)
        real = skewed[0][:, span].T
        imag = skewed[1][:, span].T
        out[tile, :BLK, :BLK] = real.astype(jnp.bfloat16)
        out[tile, :BLK, BLK:] = (-imag).astype(jnp.bfloat16)
        out[tile, BLK:, :BLK] = imag.astype(jnp.bfloat16)
        out[tile, BLK:, BLK:] = real.astype(jnp.bfloat16)


def prepare_body(place, range_taps, weights, offsets, range_out, band_out):
    toeplitz_tiles(range_taps, RANGE_TILES, HALF, range_out)
    bins = weights.shape[1]
    lane = lax.broadcasted_iota(jnp.int32, (BLK, WIDE), 1)
    for block in range(bins // BLK):
        span = slice(block * BLK, (block + 1) * BLK)
        placed = jnp.concatenate(
            [weights[:, span].astype(jnp.float32), jnp.zeros((BLK - BAND, BLK), jnp.float32)], axis=0
        )
        shifts = offsets[:, span]
        for bit in range((BAND // 2).bit_length()):
            chosen = jnp.broadcast_to((shifts >> bit) & 1, (BLK, BLK)) == 1
            placed = jnp.where(chosen, pltpu.roll(placed, 1 << bit, 0), placed)
        wide = jnp.concatenate([placed.T, jnp.zeros((BLK, BLK), jnp.float32)], axis=1)
        skewed = pltpu.roll(wide, BAND // 2, 1, stride=1, stride_axis=0)
        if block == 0:
            skewed = jnp.where((place[0] == 0) & (lane < HALF), 0.0, skewed)
        band_out[span, :] = skewed.astype(jnp.bfloat16)


def prepare(place, range_ref, weights, offsets):
    return call(
        prepare_body,
        "prepare",
        (bf16(RANGE_TILES, WIDE, WIDE), bf16(weights.shape[1], WIDE)),
        [SMEM()] + [VMEM()] * 3,
        (VMEM(),) * 2,
    )(place, range_ref, weights, offsets)


def assemble(place, echoes, near, far, out):
    blocks = echoes.shape[2] // BLK
    for block in range(blocks):
        for part in range(2):
            out[block + 1, :, part * BLK : (part + 1) * BLK] = echoes[
                part, :, block * BLK : (block + 1) * BLK
            ]

    def ends(low, high):
        out[0] = low[0]
        out[blocks + 1 :] = high[...]

    odd = place[0] % 2 == 1
    pl.when(odd)(lambda: ends(near, far))
    pl.when(jnp.logical_not(odd))(lambda: ends(far, near))


def spots(place, near, count, direct):
    me = place[1]
    if not direct:
        first = 0 if near else count
        return first, [first + i for i in range(count)]
    side = me // count if near else 1 - me // count
    return side * count, [side * count + (me % count ^ i) for i in range(count)]


def focus_range(first, groups, samples, range_tiles, bands, turned, outs):
    pulses = samples.shape[1]
    count = len(outs)
    for block in range(2 * count + 1):
        window = jnp.concatenate(
            [samples[2 * first + block + tile] for tile in range(RANGE_TILES)], axis=1
        )
        total = jnp.dot(
            window,
            range_tiles[...].reshape(RANGE_TILES * WIDE, WIDE),
            preferred_element_type=jnp.float32,
        ).astype(jnp.bfloat16)
        turned[block * BLK : (block + 1) * BLK, :] = jnp.concatenate(
            [total[:, :BLK].T, total[:, BLK:].T], axis=1
        )
    for place, out in enumerate(outs):
        group = groups[place]
        for half in range(2):
            reach = pl.multiple_of((group - first) * GROUP + half * BLK, BLK)
            start = pl.multiple_of(group * GROUP + half * BLK, BLK)
            out[half * BLK : (half + 1) * BLK, :] = jnp.dot(
                bands[pl.ds(start, BLK)],
                turned[pl.ds(reach, WIDE)],
                preferred_element_type=jnp.float32,
            ).astype(jnp.bfloat16)


def first_range_body(direct, place, echoes, near, far, range_tiles, bands, samples, *rest):
    outs, turned = rest[:-1], rest[-1]
    assemble(place, echoes, near, far, samples)
    first, groups = spots(place, not direct, len(outs), direct)
    focus_range(first, groups, samples, range_tiles, bands, turned, outs)


def second_range_body(
    direct, place, after, samples, range_tiles, bands, az_taps, az_out, *rest
):
    outs, turned = rest[:-1], rest[-1]
    toeplitz_tiles(az_taps, AZ_TILES, 0, az_out)
    first, groups = spots(place, direct, len(outs), direct)
    focus_range(first, groups, samples, range_tiles, bands, turned, outs)


def first_range(direct, place, echoes, near, far, range_tiles, bands):
    pulses = echoes.shape[1]
    count = echoes.shape[2] // GROUP // 2
    blocks = 1 + echoes.shape[2] // BLK + HEAD
    samples, *made = call(
        functools.partial(first_range_body, direct),
        "first_range",
        (bf16(blocks, pulses, WIDE),) + (bf16(GROUP, 2 * pulses),) * count,
        [SMEM()] + [VMEM()] * 5,
        (VMEM(),) * (1 + count),
        [pltpu.VMEM(((2 * count + 1) * BLK, 2 * pulses), jnp.bfloat16)],
    )(place, echoes, near, far, range_tiles, bands)
    return samples, made


def second_range(direct, place, after, samples, range_tiles, bands, azimuth_ref):
    pulses = samples.shape[1]
    count = bands.shape[0] // GROUP // 2
    az_tiles, *made = call(
        functools.partial(second_range_body, direct),
        "second_range",
        (bf16(AZ_TILES, WIDE, WIDE),) + (bf16(GROUP, 2 * pulses),) * count,
        [SMEM()] + [VMEM()] * 5,
        (VMEM(),) * (1 + count),
        [pltpu.VMEM(((2 * count + 1) * BLK, 2 * pulses), jnp.bfloat16)],
    )(place, after, samples, range_tiles, bands, azimuth_ref)
    return az_tiles, made


def focus_azimuth_body(direct, place, az_tiles, *rest):
    parts, out, rows, image, sems = rest[:-4], rest[-4], rest[-3], rest[-2], rest[-1]
    count = len(parts)
    where = range(count)
    if direct:
        where = [
            group for near in (False, True) for group in spots(place, near, count // 2, True)[1]
        ]
    bins = parts[0].shape[0]
    reach = AZ_TILES // 2
    for place, part in enumerate(parts):
        start = pl.multiple_of(where[place] * bins, bins)
        rows[pl.ds(start, bins)] = part[...]
    for block in range(count):
        low, high = max(0, reach - block), min(AZ_TILES, count + reach - block)
        window = jnp.concatenate(
            [
                rows[(block + tile - reach) * bins : (block + tile - reach + 1) * bins]
                for tile in range(low, high)
            ],
            axis=1,
        )
        total = jnp.dot(
            window,
            az_tiles[low:high].reshape((high - low) * WIDE, WIDE),
            preferred_element_type=jnp.float32,
        )
        span = pl.ds(block * BLK, BLK)
        for part in range(2):
            image[part, 0, :, span] = total[:, part * BLK : (part + 1) * BLK]
        pltpu.make_async_copy(
            image.at[:, :, :, span], out.at[:, :, :, span], sems.at[block]
        ).start()
    for block in range(count):
        span = pl.ds(block * BLK, BLK)
        pltpu.make_async_copy(
            image.at[:, :, :, span], out.at[:, :, :, span], sems.at[block]
        ).wait()


def focus_azimuth(direct, place, az_tiles, parts):
    count = len(parts)
    bins = parts[0].shape[0]
    shape = (2, 1, bins, count * BLK)
    return call(
        functools.partial(focus_azimuth_body, direct),
        "focus_azimuth",
        jax.ShapeDtypeStruct(shape, jnp.float32),
        [SMEM()] + [VMEM()] * (1 + count),
        HBM(),
        [
            pltpu.VMEM((count * bins, WIDE), jnp.bfloat16),
            pltpu.VMEM(shape, jnp.float32),
            pltpu.SemaphoreType.DMA((count,)),
        ],
    )(place, az_tiles, *parts)


def per_device(echoes, range_ref, band_weights, band_offsets, azimuth_ref):
    quarter_len = echoes.shape[2]
    peers = lax.axis_size("pulse")
    quarters = lax.axis_size("rng")
    bins = quarter_len // peers
    place = jnp.stack([lax.axis_index("rng"), lax.axis_index("pulse")]).astype(jnp.int32)

    near, far = pack(place, echoes)

    def swaps(start):
        pairs = [(i, i + 1) for i in range(start, quarters - 1, 2)]
        return pairs + [(j, i) for i, j in pairs]

    far = lax.ppermute(far, "rng", swaps(1))
    near = lax.ppermute(near, "rng", swaps(0))
    range_tiles, bands = prepare(
        place, range_ref, band_weights, band_offsets.reshape(1, quarter_len)
    )

    direct = bins == GROUP and peers & (peers - 1) == 0

    def send(pieces, start):
        return [
            lax.ppermute(piece, "pulse", [(i, i ^ k) for i in range(peers)]) if k else piece
            for k, piece in enumerate(pieces, start)
        ]

    samples, first = first_range(direct, place, echoes, near, far, range_tiles, bands)
    if direct:
        first = send(first, peers // 2)
    az_tiles, second = second_range(
        direct, place, first[0], samples, range_tiles, bands, azimuth_ref
    )
    if direct:
        return focus_azimuth(direct, place, az_tiles, first + send(second, 0))
    swapped = lax.all_to_all(
        jnp.concatenate(first + second, axis=0).reshape(peers, bins, WIDE),
        "pulse",
        split_axis=0,
        concat_axis=0,
        tiled=True,
    )
    return focus_azimuth(direct, place, az_tiles, [swapped[i] for i in range(peers)])


def solution(mesh):
    return jax.shard_map(
        per_device,
        mesh=mesh,
        in_specs=(P(None, "pulse", "rng"), P(), P(None, "rng"), P("rng"), P()),
        out_specs=P(None, "rng", "pulse", None),
        check_vma=False,
    )
```

```python
import functools

import jax
import jax.numpy as jnp
from jax import lax
from jax.experimental import pallas as pl
from jax.experimental.pallas import tpu as pltpu
from jax.sharding import PartitionSpec as P

RT = 1024
AT = 512
BAND = 64
BLK = 128
HALF = BLK // 2
WIDE = 2 * BLK
RANGE_TILES = RT // BLK + 2
AZ_TILES = AT // BLK + 1
HEAD = RT // BLK + 1
GROUP = 2 * BLK
LIMIT = 24 * 1024 * 1024

VMEM = functools.partial(pl.BlockSpec, memory_space=pltpu.VMEM)
HBM = functools.partial(pl.BlockSpec, memory_space=pltpu.HBM)


def call(body, name, out_shape, in_specs, out_specs, scratch_shapes=()):
    return pl.pallas_call(
        body,
        out_shape=out_shape,
        in_specs=in_specs,
        out_specs=out_specs,
        scratch_shapes=scratch_shapes,
        compiler_params=pltpu.CompilerParams(vmem_limit_bytes=LIMIT),
        cost_estimate=pl.CostEstimate(flops=0, bytes_accessed=0, transcendentals=0),
        name=name,
    )


def bf16(*shape):
    return jax.ShapeDtypeStruct(shape, jnp.bfloat16)


def pack_body(echoes, near, far):
    odd = lax.axis_index("rng") % 2 == 1

    def fill(down, up):
        for part in range(2):
            lanes = slice(part * BLK, (part + 1) * BLK)
            for block in range(HEAD):
                down[block, :, lanes] = echoes[part, :, block * BLK : (block + 1) * BLK]
            up[0, :, lanes] = echoes[part, :, echoes.shape[2] - BLK :]

    pl.when(odd)(lambda: fill(near, far))
    pl.when(jnp.logical_not(odd))(lambda: fill(far, near))


def pack(echoes):
    return call(
        pack_body,
        "pack",
        (bf16(HEAD, echoes.shape[1], WIDE),) * 2,
        [VMEM()],
        (VMEM(),) * 2,
    )(echoes)


OFFSET_ROW = BAND
RANGE_ROW = BAND + 8
AZ_ROW = BAND + 16
TABLE_ROWS = BAND + 24


def join_small(weights, offsets, range_ref, azimuth_ref):
    bins = weights.shape[1]

    def rows(value):
        return jnp.pad(value, ((0, 8 - value.shape[0]), (0, bins - value.shape[1])))

    return jnp.concatenate(
        [weights, rows(offsets.astype(jnp.bfloat16)[None]), rows(range_ref), rows(azimuth_ref)],
        axis=0,
    )


def toeplitz_tiles(table, start, tap_total, tiles, shift, out):
    width = (tiles + 1) * BLK
    skewed = []
    for part in range(2):
        row = jnp.concatenate(
            [
                jnp.zeros((1, BLK), jnp.float32),
                table[start : start + 8, :tap_total].astype(jnp.float32)[part : part + 1],
                jnp.zeros((1, width - BLK - tap_total), jnp.float32),
            ],
            axis=1,
        )
        row = jnp.broadcast_to(row, (BLK, width))
        skewed.append(pltpu.roll(row, shift, 1, stride=1, stride_axis=0))
    for tile in range(tiles):
        span = slice((tile + 1) * BLK, (tile + 2) * BLK)
        real = skewed[0][:, span].T
        imag = skewed[1][:, span].T
        out[tile, :BLK, :BLK] = real.astype(jnp.bfloat16)
        out[tile, :BLK, BLK:] = (-imag).astype(jnp.bfloat16)
        out[tile, BLK:, :BLK] = imag.astype(jnp.bfloat16)
        out[tile, BLK:, BLK:] = real.astype(jnp.bfloat16)


def prepare_body(table, range_out, band_out):
    toeplitz_tiles(table, RANGE_ROW, RT, RANGE_TILES, HALF, range_out)
    lowest = lax.axis_index("rng") == 0
    lane = lax.broadcasted_iota(jnp.int32, (BLK, WIDE), 1)
    for block in range(table.shape[1] // BLK):
        span = slice(block * BLK, (block + 1) * BLK)
        placed = jnp.concatenate(
            [
                table[:BAND, span].astype(jnp.float32),
                jnp.zeros((BLK - BAND, BLK), jnp.float32),
            ],
            axis=0,
        )
        shifts = table[OFFSET_ROW : OFFSET_ROW + 8, span].astype(jnp.float32).astype(jnp.int32)[:1]
        for bit in range((BAND // 2).bit_length()):
            chosen = jnp.broadcast_to((shifts >> bit) & 1, (BLK, BLK)) == 1
            placed = jnp.where(chosen, pltpu.roll(placed, 1 << bit, 0), placed)
        wide = jnp.concatenate([placed.T, jnp.zeros((BLK, BLK), jnp.float32)], axis=1)
        skewed = pltpu.roll(wide, BAND // 2, 1, stride=1, stride_axis=0)
        if block == 0:
            skewed = jnp.where(lowest & (lane < HALF), 0.0, skewed)
        band_out[span, :] = skewed.astype(jnp.bfloat16)


def prepare(table):
    return call(
        prepare_body,
        "prepare",
        (bf16(RANGE_TILES, WIDE, WIDE), bf16(table.shape[1], WIDE)),
        [VMEM()],
        (VMEM(),) * 2,
    )(table)


def assemble(echoes, near, far, out):
    blocks = echoes.shape[2] // BLK
    for block in range(blocks):
        for part in range(2):
            out[block + 1, :, part * BLK : (part + 1) * BLK] = echoes[
                part, :, block * BLK : (block + 1) * BLK
            ]

    def ends(low, high):
        out[0] = low[0]
        out[blocks + 1 :] = high[...]

    odd = lax.axis_index("rng") % 2 == 1
    pl.when(odd)(lambda: ends(near, far))
    pl.when(jnp.logical_not(odd))(lambda: ends(far, near))


def compress(samples, range_tiles, block):
    window = jnp.concatenate([samples[block + tile] for tile in range(RANGE_TILES)], axis=1)
    total = jnp.dot(
        window,
        range_tiles[...].reshape(RANGE_TILES * WIDE, WIDE),
        preferred_element_type=jnp.float32,
    ).astype(jnp.bfloat16)
    return jnp.concatenate([total[:, :BLK].T, total[:, BLK:].T], axis=1)


def migrate(bands, turned, first, place):
    reach = pl.multiple_of(place * BLK, BLK)
    start = pl.multiple_of((first + place) * BLK, BLK)
    return jnp.dot(
        bands[pl.ds(start, BLK)], turned[pl.ds(reach, WIDE)], preferred_element_type=jnp.float32
    ).astype(jnp.bfloat16)


def groups_of(first, count, spots, samples, range_tiles, bands, turned, outs):
    for block in range(count + 1):
        turned[block * BLK : (block + 1) * BLK, :] = compress(samples, range_tiles, first + block)
    for spot, out in zip(spots, outs):
        for block in range(GROUP // BLK):
            out[block * BLK : (block + 1) * BLK, :] = migrate(
                bands, turned, first, spot * (GROUP // BLK) + block
            )


def far_pair(step, samples, range_tiles, bands, turned, outs):
    me = lax.axis_index("pulse")
    first = 4 * (me // 2 ^ step)
    groups_of(first, 4, [me % 2, me % 2 ^ 1], samples, range_tiles, bands, turned, outs)


def first_far_body(step, echoes, near, far, range_tiles, bands, samples, *rest):
    assemble(echoes, near, far, samples)
    far_pair(step, samples, range_tiles, bands, rest[-1], rest[:-1])


def first_far(step, echoes, near, far, range_tiles, bands):
    pulses = echoes.shape[1]
    blocks = 1 + echoes.shape[2] // BLK + HEAD
    samples, *made = call(
        functools.partial(first_far_body, step),
        "first_far",
        (bf16(blocks, pulses, WIDE),) + (bf16(GROUP, 2 * pulses),) * 2,
        [VMEM()] * 5,
        (VMEM(),) * 3,
        [pltpu.VMEM((5 * BLK, 2 * pulses), jnp.bfloat16)],
    )(echoes, near, far, range_tiles, bands)
    return samples, made


def rest_body(step, count, after, samples, range_tiles, bands, table, *rest):
    *outs, az_out, turned = rest
    far_pair(step, samples, range_tiles, bands, turned, outs[:2])
    me = lax.axis_index("pulse")
    groups_of(
        me // count * count * (GROUP // BLK),
        count * (GROUP // BLK),
        [me % count ^ k for k in range(count)],
        samples,
        range_tiles,
        bands,
        turned.at[pl.ds(5 * BLK, (count * (GROUP // BLK) + 1) * BLK)],
        outs[2:],
    )
    toeplitz_tiles(table, AZ_ROW, AT, AZ_TILES, 0, az_out)


def rest_range(step, after, samples, range_tiles, bands, table):
    pulses = samples.shape[1]
    count = bands.shape[0] // GROUP // 2
    *made, az_tiles = call(
        functools.partial(rest_body, step, count),
        "rest_range",
        (bf16(GROUP, 2 * pulses),) * (2 + count) + (bf16(AZ_TILES, WIDE, WIDE),),
        [VMEM()] * 5,
        (VMEM(),) * (3 + count),
        [pltpu.VMEM(((count * (GROUP // BLK) + 6) * BLK, 2 * pulses), jnp.bfloat16)],
    )(after, samples, range_tiles, bands, table)
    return made[:2], made[2:], az_tiles


def gate_body(*refs):
    pass


def gate(values, after):
    whole = pl.BlockSpec(memory_space=pl.ANY)
    return pl.pallas_call(
        gate_body,
        out_shape=tuple(jax.ShapeDtypeStruct(value.shape, value.dtype) for value in values),
        in_specs=[whole] * (len(values) + len(after)),
        out_specs=(whole,) * len(values),
        input_output_aliases={i: i for i in range(len(values))},
        compiler_params=pltpu.CompilerParams(vmem_limit_bytes=LIMIT),
        name="gate",
    )(*values, *after)


def whole_body(count, echoes, near, far, range_tiles, bands, table, out, az_out, samples, turned):
    assemble(echoes, near, far, samples)
    for block in range(count + 1):
        turned[block * BLK : (block + 1) * BLK, :] = compress(samples, range_tiles, block)
    for block in range(count):
        out[block * BLK : (block + 1) * BLK, :] = migrate(bands, turned, 0, block)
    toeplitz_tiles(table, AZ_ROW, AT, AZ_TILES, 0, az_out)


def whole_quarter(echoes, near, far, range_tiles, bands, table):
    pulses = echoes.shape[1]
    count = bands.shape[0] // BLK
    return call(
        functools.partial(whole_body, count),
        "whole_quarter",
        (bf16(count * BLK, 2 * pulses), bf16(AZ_TILES, WIDE, WIDE)),
        [VMEM()] * 6,
        (VMEM(),) * 2,
        [
            pltpu.VMEM((1 + count + HEAD, pulses, WIDE), jnp.bfloat16),
            pltpu.VMEM(((count + 1) * BLK, 2 * pulses), jnp.bfloat16),
        ],
    )(echoes, near, far, range_tiles, bands, table)


def focus_azimuth_body(steps, count, az_tiles, *rest):
    parts, out, rows, image, sems = rest[:-4], rest[-4], rest[-3], rest[-2], rest[-1]
    bins = image.shape[2]
    reach = AZ_TILES // 2
    me = lax.axis_index("pulse")
    if steps:
        starts = [me ^ step for step in steps]
    else:
        starts = [0]
    for start, part in zip(starts, parts):
        rows[pl.ds(pl.multiple_of(start * bins, bins), part.shape[0])] = part[...]
    for block in range(count):
        low, high = max(0, reach - block), min(AZ_TILES, count + reach - block)
        window = jnp.concatenate(
            [
                rows[(block + tile - reach) * bins : (block + tile - reach + 1) * bins]
                for tile in range(low, high)
            ],
            axis=1,
        )
        total = jnp.dot(
            window,
            az_tiles[low:high].reshape((high - low) * WIDE, WIDE),
            preferred_element_type=jnp.float32,
        )
        span = pl.ds(block * BLK, BLK)
        for part in range(2):
            image[part, 0, :, span] = total[:, part * BLK : (part + 1) * BLK]
        pltpu.make_async_copy(
            image.at[:, :, :, span], out.at[:, :, :, span], sems.at[block]
        ).start()
    for block in range(count):
        span = pl.ds(block * BLK, BLK)
        pltpu.make_async_copy(
            image.at[:, :, :, span], out.at[:, :, :, span], sems.at[block]
        ).wait()


def focus_azimuth(steps, az_tiles, parts):
    count = lax.axis_size("pulse")
    bins = sum(part.shape[0] for part in parts) // count
    shape = (2, 1, bins, count * BLK)
    return call(
        functools.partial(focus_azimuth_body, steps, count),
        "focus_azimuth",
        jax.ShapeDtypeStruct(shape, jnp.float32),
        [VMEM()] * (1 + len(parts)),
        HBM(),
        [
            pltpu.VMEM((count * bins, WIDE), jnp.bfloat16),
            pltpu.VMEM(shape, jnp.float32),
            pltpu.SemaphoreType.DMA((count,)),
        ],
    )(az_tiles, *parts)


def per_device(echoes, range_ref, band_weights, band_offsets, azimuth_ref):
    quarter_len = echoes.shape[2]
    peers = lax.axis_size("pulse")
    quarters = lax.axis_size("rng")
    bins = quarter_len // peers
    near, far = pack(echoes)

    def swaps(start):
        pairs = [(i, i + 1) for i in range(start, quarters - 1, 2)]
        return pairs + [(j, i) for i, j in pairs]

    far = lax.ppermute(far, "rng", swaps(1))
    near = lax.ppermute(near, "rng", swaps(0))
    table = join_small(band_weights, band_offsets, range_ref, azimuth_ref)
    range_tiles, bands = prepare(table)

    if bins != GROUP or peers != 8:
        mine, az_tiles = whole_quarter(echoes, near, far, range_tiles, bands, table)
        swapped = lax.all_to_all(
            mine.reshape(peers, bins, WIDE), "pulse", split_axis=0, concat_axis=0, tiled=True
        )
        return focus_azimuth(None, az_tiles, [swapped.reshape(mine.shape)])

    half = peers // 2

    def send(piece, k):
        return lax.ppermute(piece, "pulse", [(i, i ^ k) for i in range(peers)])

    samples, made = first_far(half // 2, echoes, near, far, range_tiles, bands)
    parts = [send(piece, half + k) for k, piece in enumerate(made)]
    made, mine, az_tiles = rest_range(half // 2 + 1, made[0], samples, range_tiles, bands, table)
    more = [send(piece, half + 2 + k) for k, piece in enumerate(made)]
    held = gate(mine[1:], parts)
    mine = mine[:1] + [send(piece, 1 + k) for k, piece in enumerate(held)]
    return focus_azimuth(
        list(range(half)) + list(range(half, peers)), az_tiles, mine + parts + more
    )


def solution(mesh):
    return jax.shard_map(
        per_device,
        mesh=mesh,
        in_specs=(P(None, "pulse", "rng"), P(), P(None, "rng"), P("rng"), P()),
        out_specs=P(None, "rng", "pulse", None),
        check_vma=False,
    )
```

```python
import functools

import jax
import jax.numpy as jnp
from jax import lax
from jax.experimental import pallas as pl
from jax.experimental.pallas import tpu as pltpu
from jax.sharding import PartitionSpec as P

RT = 1024
AT = 512
BAND = 64
BLK = 128
HALF = BLK // 2
WIDE = 2 * BLK
RANGE_TILES = RT // BLK + 2
AZ_TILES = AT // BLK + 1
HEAD = RT // BLK + 1
GROUP = 2 * BLK
LIMIT = 24 * 1024 * 1024
PACK_FLOPS = 2 * 10**9

VMEM = functools.partial(pl.BlockSpec, memory_space=pltpu.VMEM)
HBM = functools.partial(pl.BlockSpec, memory_space=pltpu.HBM)


def call(body, name, out_shape, in_specs, out_specs, scratch_shapes=(), flops=0):
    return pl.pallas_call(
        body,
        out_shape=out_shape,
        in_specs=in_specs,
        out_specs=out_specs,
        scratch_shapes=scratch_shapes,
        compiler_params=pltpu.CompilerParams(vmem_limit_bytes=LIMIT),
        cost_estimate=pl.CostEstimate(flops=flops, bytes_accessed=0, transcendentals=0),
        name=name,
    )


def bf16(*shape):
    return jax.ShapeDtypeStruct(shape, jnp.bfloat16)


def pack_body(echoes, near, far):
    odd = lax.axis_index("rng") % 2 == 1

    def fill(down, up):
        for part in range(2):
            lanes = slice(part * BLK, (part + 1) * BLK)
            for block in range(HEAD):
                down[block, :, lanes] = echoes[part, :, block * BLK : (block + 1) * BLK]
            up[0, :, lanes] = echoes[part, :, echoes.shape[2] - BLK :]

    pl.when(odd)(lambda: fill(near, far))
    pl.when(jnp.logical_not(odd))(lambda: fill(far, near))


def pack(echoes):
    return call(
        pack_body,
        "pack",
        (bf16(HEAD, echoes.shape[1], WIDE),) * 2,
        [VMEM()],
        (VMEM(),) * 2,
        flops=PACK_FLOPS,
    )(echoes)


def toeplitz_tiles(taps, tiles, shift, out):
    width = (tiles + 1) * BLK
    tap_total = taps.shape[1]
    skewed = []
    for part in range(2):
        row = jnp.concatenate(
            [
                jnp.zeros((1, BLK), jnp.float32),
                taps[part : part + 1, :].astype(jnp.float32),
                jnp.zeros((1, width - BLK - tap_total), jnp.float32),
            ],
            axis=1,
        )
        row = jnp.broadcast_to(row, (BLK, width))
        skewed.append(pltpu.roll(row, shift, 1, stride=1, stride_axis=0))
    for tile in range(tiles):
        span = slice((tile + 1) * BLK, (tile + 2) * BLK)
        real = skewed[0][:, span].T
        imag = skewed[1][:, span].T
        out[tile, :BLK, :BLK] = real.astype(jnp.bfloat16)
        out[tile, :BLK, BLK:] = (-imag).astype(jnp.bfloat16)
        out[tile, BLK:, :BLK] = imag.astype(jnp.bfloat16)
        out[tile, BLK:, BLK:] = real.astype(jnp.bfloat16)


def prepare_body(range_ref, weights, offsets, range_out, band_out):
    toeplitz_tiles(range_ref, RANGE_TILES, HALF, range_out)
    lowest = lax.axis_index("rng") == 0
    lane = lax.broadcasted_iota(jnp.int32, (BLK, WIDE), 1)
    for block in range(weights.shape[1] // BLK):
        span = slice(block * BLK, (block + 1) * BLK)
        placed = jnp.concatenate(
            [
                weights[:, span].astype(jnp.float32),
                jnp.zeros((BLK - BAND, BLK), jnp.float32),
            ],
            axis=0,
        )
        shifts = offsets[block : block + 1, :]
        for bit in range((BAND // 2).bit_length()):
            chosen = jnp.broadcast_to((shifts >> bit) & 1, (BLK, BLK)) == 1
            placed = jnp.where(chosen, pltpu.roll(placed, 1 << bit, 0), placed)
        wide = jnp.concatenate([placed.T, jnp.zeros((BLK, BLK), jnp.float32)], axis=1)
        skewed = pltpu.roll(wide, BAND // 2, 1, stride=1, stride_axis=0)
        if block == 0:
            skewed = jnp.where(lowest & (lane < HALF), 0.0, skewed)
        band_out[span, :] = skewed.astype(jnp.bfloat16)


def prepare(range_ref, weights, offsets):
    return call(
        prepare_body,
        "prepare",
        (bf16(RANGE_TILES, WIDE, WIDE), bf16(weights.shape[1], WIDE)),
        [VMEM()] * 3,
        (VMEM(),) * 2,
    )(range_ref, weights, offsets.reshape(-1, BLK))


def assemble(echoes, near, far, out):
    blocks = echoes.shape[2] // BLK
    for block in range(blocks):
        for part in range(2):
            out[block + 1, :, part * BLK : (part + 1) * BLK] = echoes[
                part, :, block * BLK : (block + 1) * BLK
            ]

    def ends(low, high):
        out[0] = low[0]
        out[blocks + 1 :] = high[...]

    odd = lax.axis_index("rng") % 2 == 1
    pl.when(odd)(lambda: ends(near, far))
    pl.when(jnp.logical_not(odd))(lambda: ends(far, near))


def compress(samples, range_tiles, block):
    window = jnp.concatenate([samples[block + tile] for tile in range(RANGE_TILES)], axis=1)
    total = jnp.dot(
        window,
        range_tiles[...].reshape(RANGE_TILES * WIDE, WIDE),
        preferred_element_type=jnp.float32,
    ).astype(jnp.bfloat16)
    return jnp.concatenate([total[:, :BLK].T, total[:, BLK:].T], axis=1)


def migrate(bands, turned, first, place):
    reach = pl.multiple_of(place * BLK, BLK)
    start = pl.multiple_of((first + place) * BLK, BLK)
    return jnp.dot(
        bands[pl.ds(start, BLK)], turned[pl.ds(reach, WIDE)], preferred_element_type=jnp.float32
    ).astype(jnp.bfloat16)


def groups_of(first, count, spots, samples, range_tiles, bands, turned, outs):
    for block in range(count + 1):
        turned[block * BLK : (block + 1) * BLK, :] = compress(samples, range_tiles, first + block)
    rows = [out.at[pl.ds(i, GROUP)] for out in outs for i in range(0, out.shape[0], GROUP)]
    for spot, out in zip(spots, rows):
        for block in range(GROUP // BLK):
            out[block * BLK : (block + 1) * BLK, :] = migrate(
                bands, turned, first, spot * (GROUP // BLK) + block
            )


def far_pair(step, samples, range_tiles, bands, turned, outs):
    me = lax.axis_index("pulse")
    first = 4 * (me // 2 ^ step)
    groups_of(first, 4, [me % 2, me % 2 ^ 1], samples, range_tiles, bands, turned, outs)


def first_far_body(step, echoes, near, far, range_tiles, bands, samples, *rest):
    assemble(echoes, near, far, samples)
    far_pair(step, samples, range_tiles, bands, rest[-1], rest[:-1])


def first_far(step, echoes, near, far, range_tiles, bands):
    pulses = echoes.shape[1]
    blocks = 1 + echoes.shape[2] // BLK + HEAD
    samples, *made = call(
        functools.partial(first_far_body, step),
        "first_far",
        (bf16(blocks, pulses, WIDE),) + (bf16(GROUP, 2 * pulses),) * 2,
        [VMEM()] * 5,
        (VMEM(),) * 3,
        [pltpu.VMEM((5 * BLK, 2 * pulses), jnp.bfloat16)],
    )(echoes, near, far, range_tiles, bands)
    return samples, made


def next_far_body(step, samples, range_tiles, bands, *rest):
    far_pair(step, samples, range_tiles, bands, rest[-1], rest[:-1])


def next_far(step, samples, range_tiles, bands):
    pulses = samples.shape[1]
    return call(
        functools.partial(next_far_body, step),
        "next_far",
        (bf16(GROUP, 2 * pulses),) * 2,
        [VMEM()] * 3,
        (VMEM(),) * 2,
        [pltpu.VMEM((5 * BLK, 2 * pulses), jnp.bfloat16)],
    )(samples, range_tiles, bands)


def near_body(count, after, samples, range_tiles, bands, az_taps, out, az_out, turned):
    me = lax.axis_index("pulse")
    groups_of(
        me // count * count * (GROUP // BLK),
        count * (GROUP // BLK),
        list(range(count)),
        samples,
        range_tiles,
        bands,
        turned,
        [out],
    )
    toeplitz_tiles(az_taps, AZ_TILES, 0, az_out)


def near_half(after, samples, range_tiles, bands, azimuth_ref):
    pulses = samples.shape[1]
    count = bands.shape[0] // GROUP // 2
    return call(
        functools.partial(near_body, count),
        "near_half",
        (bf16(count * GROUP, 2 * pulses), bf16(AZ_TILES, WIDE, WIDE)),
        [VMEM()] * 5,
        (VMEM(),) * 2,
        [pltpu.VMEM(((count * (GROUP // BLK) + 1) * BLK, 2 * pulses), jnp.bfloat16)],
    )(after, samples, range_tiles, bands, azimuth_ref)


def gate_body(*refs):
    pass


def gate(values, after=(), flops=0):
    whole = pl.BlockSpec(memory_space=pl.ANY)
    values = list(values)
    return pl.pallas_call(
        gate_body,
        out_shape=tuple(jax.ShapeDtypeStruct(value.shape, value.dtype) for value in values),
        in_specs=[whole] * (len(values) + len(after)),
        out_specs=(whole,) * len(values),
        input_output_aliases={i: i for i in range(len(values))},
        compiler_params=pltpu.CompilerParams(vmem_limit_bytes=LIMIT),
        cost_estimate=pl.CostEstimate(flops=flops, bytes_accessed=0, transcendentals=0),
        name="gate",
    )(*values, *after)


def whole_body(count, echoes, near, far, range_tiles, bands, az_taps, out, az_out, samples, turned):
    assemble(echoes, near, far, samples)
    for block in range(count + 1):
        turned[block * BLK : (block + 1) * BLK, :] = compress(samples, range_tiles, block)
    for block in range(count):
        out[block * BLK : (block + 1) * BLK, :] = migrate(bands, turned, 0, block)
    toeplitz_tiles(az_taps, AZ_TILES, 0, az_out)


def whole_quarter(echoes, near, far, range_tiles, bands, azimuth_ref):
    pulses = echoes.shape[1]
    count = bands.shape[0] // BLK
    return call(
        functools.partial(whole_body, count),
        "whole_quarter",
        (bf16(count * BLK, 2 * pulses), bf16(AZ_TILES, WIDE, WIDE)),
        [VMEM()] * 6,
        (VMEM(),) * 2,
        [
            pltpu.VMEM((1 + count + HEAD, pulses, WIDE), jnp.bfloat16),
            pltpu.VMEM(((count + 1) * BLK, 2 * pulses), jnp.bfloat16),
        ],
    )(echoes, near, far, range_tiles, bands, azimuth_ref)


def focus_azimuth_body(steps, count, az_tiles, *rest):
    parts, out, rows, image, sems = rest[:-4], rest[-4], rest[-3], rest[-2], rest[-1]
    bins = image.shape[2]
    reach = AZ_TILES // 2
    me = lax.axis_index("pulse")
    if steps:
        half = steps[0]
        start = pl.multiple_of(me // half * half * bins, half * bins)
        rows[pl.ds(start, half * bins)] = parts[0][...]
        for part, step in zip(parts[1:], steps[1:]):
            rows[pl.ds(pl.multiple_of((me ^ step) * bins, bins), bins)] = part[...]
    else:
        rows[...] = parts[0][...]
    for block in range(count):
        low, high = max(0, reach - block), min(AZ_TILES, count + reach - block)
        window = jnp.concatenate(
            [
                rows[(block + tile - reach) * bins : (block + tile - reach + 1) * bins]
                for tile in range(low, high)
            ],
            axis=1,
        )
        total = jnp.dot(
            window,
            az_tiles[low:high].reshape((high - low) * WIDE, WIDE),
            preferred_element_type=jnp.float32,
        )
        span = pl.ds(block * BLK, BLK)
        for part in range(2):
            image[part, 0, :, span] = total[:, part * BLK : (part + 1) * BLK]
        pltpu.make_async_copy(
            image.at[:, :, :, span], out.at[:, :, :, span], sems.at[block]
        ).start()
    for block in range(count):
        span = pl.ds(block * BLK, BLK)
        pltpu.make_async_copy(
            image.at[:, :, :, span], out.at[:, :, :, span], sems.at[block]
        ).wait()


def focus_azimuth(steps, bins, az_tiles, parts):
    count = lax.axis_size("pulse")
    shape = (2, 1, bins, count * BLK)
    return call(
        functools.partial(focus_azimuth_body, steps, count),
        "focus_azimuth",
        jax.ShapeDtypeStruct(shape, jnp.float32),
        [VMEM()] * (1 + len(parts)),
        HBM(),
        [
            pltpu.VMEM((count * bins, WIDE), jnp.bfloat16),
            pltpu.VMEM(shape, jnp.float32),
            pltpu.SemaphoreType.DMA((count,)),
        ],
    )(az_tiles, *parts)


def per_device(echoes, range_ref, band_weights, band_offsets, azimuth_ref):
    quarter_len = echoes.shape[2]
    peers = lax.axis_size("pulse")
    quarters = lax.axis_size("rng")
    bins = quarter_len // peers
    near, far = pack(echoes)

    def swaps(start):
        pairs = [(i, i + 1) for i in range(start, quarters - 1, 2)]
        return pairs + [(j, i) for i, j in pairs]

    far = lax.ppermute(far, "rng", swaps(1))
    near = lax.ppermute(near, "rng", swaps(0))
    range_tiles, bands = prepare(range_ref, band_weights, band_offsets)

    if bins != GROUP or peers != 8:
        mine, az_tiles = whole_quarter(echoes, near, far, range_tiles, bands, azimuth_ref)
        swapped = lax.all_to_all(
            mine.reshape(peers, bins, WIDE), "pulse", split_axis=0, concat_axis=0, tiled=True
        )
        return focus_azimuth(None, bins, az_tiles, [swapped.reshape(mine.shape)])

    half = peers // 2

    def send(piece, k):
        return lax.ppermute(piece, "pulse", [(i, i ^ k) for i in range(peers)])

    samples, made = first_far(half // 2, echoes, near, far, range_tiles, bands)
    parts = [send(piece, half + k) for k, piece in enumerate(made)]
    made = next_far(half // 2 + 1, samples, range_tiles, bands)
    parts += [send(piece, half + 2 + k) for k, piece in enumerate(made)]
    mine, az_tiles = near_half(made[0], samples, range_tiles, bands, azimuth_ref)
    mine = lax.all_to_all(
        mine.reshape(half, bins, WIDE),
        "pulse",
        split_axis=0,
        concat_axis=0,
        axis_index_groups=[list(range(half)), list(range(half, peers))],
        tiled=True,
    ).reshape(mine.shape)
    parts = gate(gate(parts[:2], (), 500000000) + tuple(parts[2:]), (), 20000000000)
    return focus_azimuth([half] + list(range(half, peers)), bins, az_tiles, [mine, *parts])


def solution(mesh):
    return jax.shard_map(
        per_device,
        mesh=mesh,
        in_specs=(P(None, "pulse", "rng"), P(), P(None, "rng"), P("rng"), P()),
        out_specs=P(None, "rng", "pulse", None),
        check_vma=False,
    )
```

```python
import functools

import jax
import jax.numpy as jnp
from jax import lax
from jax.experimental import pallas as pl
from jax.experimental.pallas import tpu as pltpu
from jax.sharding import PartitionSpec as P

RT = 1024
AT = 512
BAND = 64
BLK = 128
HALF = BLK // 2
WIDE = 2 * BLK
RANGE_TILES = RT // BLK + 2
AZ_TILES = AT // BLK + 1
HEAD = RT // BLK + 1
GROUP = 2 * BLK
LIMIT = 24 * 1024 * 1024
PACK_FLOPS = 2 * 10**9

VMEM = functools.partial(pl.BlockSpec, memory_space=pltpu.VMEM)
HBM = functools.partial(pl.BlockSpec, memory_space=pltpu.HBM)


def call(body, name, out_shape, in_specs, out_specs, scratch_shapes=(), flops=0):
    return pl.pallas_call(
        body,
        out_shape=out_shape,
        in_specs=in_specs,
        out_specs=out_specs,
        scratch_shapes=scratch_shapes,
        compiler_params=pltpu.CompilerParams(vmem_limit_bytes=LIMIT),
        cost_estimate=pl.CostEstimate(flops=flops, bytes_accessed=0, transcendentals=0),
        name=name,
    )


def bf16(*shape):
    return jax.ShapeDtypeStruct(shape, jnp.bfloat16)


def pack_body(echoes, near, far):
    odd = lax.axis_index("rng") % 2 == 1

    def fill(down, up):
        for part in range(2):
            lanes = slice(part * BLK, (part + 1) * BLK)
            for block in range(HEAD):
                down[block, :, lanes] = echoes[part, :, block * BLK : (block + 1) * BLK]
            up[0, :, lanes] = echoes[part, :, echoes.shape[2] - BLK :]

    pl.when(odd)(lambda: fill(near, far))
    pl.when(jnp.logical_not(odd))(lambda: fill(far, near))


def pack(echoes):
    return call(
        pack_body,
        "pack",
        (bf16(HEAD, echoes.shape[1], WIDE),) * 2,
        [VMEM()],
        (VMEM(),) * 2,
        flops=PACK_FLOPS,
    )(echoes)


def toeplitz_tiles(taps, tiles, shift, out):
    width = (tiles + 1) * BLK
    tap_total = taps.shape[1]
    skewed = []
    for part in range(2):
        row = jnp.concatenate(
            [
                jnp.zeros((1, BLK), jnp.float32),
                taps[part : part + 1, :].astype(jnp.float32),
                jnp.zeros((1, width - BLK - tap_total), jnp.float32),
            ],
            axis=1,
        )
        row = jnp.broadcast_to(row, (BLK, width))
        skewed.append(pltpu.roll(row, shift, 1, stride=1, stride_axis=0))
    for tile in range(tiles):
        span = slice((tile + 1) * BLK, (tile + 2) * BLK)
        real = skewed[0][:, span].T
        imag = skewed[1][:, span].T
        out[tile, :BLK, :BLK] = real.astype(jnp.bfloat16)
        out[tile, :BLK, BLK:] = (-imag).astype(jnp.bfloat16)
        out[tile, BLK:, :BLK] = imag.astype(jnp.bfloat16)
        out[tile, BLK:, BLK:] = real.astype(jnp.bfloat16)


def prepare_body(range_ref, weights, offsets, range_out, band_out):
    toeplitz_tiles(range_ref, RANGE_TILES, HALF, range_out)
    lowest = lax.axis_index("rng") == 0
    lane = lax.broadcasted_iota(jnp.int32, (BLK, WIDE), 1)
    for block in range(weights.shape[1] // BLK):
        span = slice(block * BLK, (block + 1) * BLK)
        placed = jnp.concatenate(
            [
                weights[:, span].astype(jnp.float32),
                jnp.zeros((BLK - BAND, BLK), jnp.float32),
            ],
            axis=0,
        )
        shifts = offsets[block : block + 1, :]
        for bit in range((BAND // 2).bit_length()):
            chosen = jnp.broadcast_to((shifts >> bit) & 1, (BLK, BLK)) == 1
            placed = jnp.where(chosen, pltpu.roll(placed, 1 << bit, 0), placed)
        wide = jnp.concatenate([placed.T, jnp.zeros((BLK, BLK), jnp.float32)], axis=1)
        skewed = pltpu.roll(wide, BAND // 2, 1, stride=1, stride_axis=0)
        if block == 0:
            skewed = jnp.where(lowest & (lane < HALF), 0.0, skewed)
        band_out[span, :] = skewed.astype(jnp.bfloat16)


def prepare(range_ref, weights, offsets):
    return call(
        prepare_body,
        "prepare",
        (bf16(RANGE_TILES, WIDE, WIDE), bf16(weights.shape[1], WIDE)),
        [VMEM()] * 3,
        (VMEM(),) * 2,
    )(range_ref, weights, offsets.reshape(-1, BLK))


def assemble(echoes, near, far, out):
    blocks = echoes.shape[2] // BLK
    for block in range(blocks):
        for part in range(2):
            out[block + 1, :, part * BLK : (part + 1) * BLK] = echoes[
                part, :, block * BLK : (block + 1) * BLK
            ]

    def ends(low, high):
        out[0] = low[0]
        out[blocks + 1 :] = high[...]

    odd = lax.axis_index("rng") % 2 == 1
    pl.when(odd)(lambda: ends(near, far))
    pl.when(jnp.logical_not(odd))(lambda: ends(far, near))


def compress(samples, range_tiles, block):
    window = jnp.concatenate([samples[block + tile] for tile in range(RANGE_TILES)], axis=1)
    total = jnp.dot(
        window,
        range_tiles[...].reshape(RANGE_TILES * WIDE, WIDE),
        preferred_element_type=jnp.float32,
    ).astype(jnp.bfloat16)
    return jnp.concatenate([total[:, :BLK].T, total[:, BLK:].T], axis=1)


def migrate(bands, turned, first, place):
    reach = pl.multiple_of(place * BLK, BLK)
    start = pl.multiple_of((first + place) * BLK, BLK)
    return jnp.dot(
        bands[pl.ds(start, BLK)], turned[pl.ds(reach, WIDE)], preferred_element_type=jnp.float32
    ).astype(jnp.bfloat16)


def groups_of(first, count, spots, samples, range_tiles, bands, turned, outs):
    for block in range(count + 1):
        turned[block * BLK : (block + 1) * BLK, :] = compress(samples, range_tiles, first + block)
    rows = [out.at[pl.ds(i, GROUP)] for out in outs for i in range(0, out.shape[0], GROUP)]
    for spot, out in zip(spots, rows):
        for block in range(GROUP // BLK):
            out[block * BLK : (block + 1) * BLK, :] = migrate(
                bands, turned, first, spot * (GROUP // BLK) + block
            )


def group_sends(steps, samples, range_tiles, bands, turned, outs):
    me = lax.axis_index("pulse")
    blocks = GROUP // BLK
    if len(steps) == 1:
        first, spots = blocks * (me ^ steps[0]), [0]
    else:
        first, spots = 2 * blocks * (me // 2 ^ steps[0] // 2), [me % 2 ^ k % 2 for k in steps]
    groups_of(first, blocks * len(steps), spots, samples, range_tiles, bands, turned, outs)


def first_range_body(steps, echoes, near, far, range_tiles, bands, samples, *rest):
    assemble(echoes, near, far, samples)
    group_sends(steps, samples, range_tiles, bands, rest[-1], rest[:-1])


def first_range(steps, echoes, near, far, range_tiles, bands):
    pulses = echoes.shape[1]
    blocks = 1 + echoes.shape[2] // BLK + HEAD
    samples, *made = call(
        functools.partial(first_range_body, steps),
        "first_range",
        (bf16(blocks, pulses, WIDE),) + (bf16(GROUP, 2 * pulses),) * 2,
        [VMEM()] * 5,
        (VMEM(),) * 3,
        [pltpu.VMEM((5 * BLK, 2 * pulses), jnp.bfloat16)],
    )(echoes, near, far, range_tiles, bands)
    return samples, made


def next_range_body(steps, after, samples, range_tiles, bands, *rest):
    *outs, turned = rest
    done = row = 0
    for some in steps:
        size = len(some) * (GROUP // BLK) + 1
        group_sends(
            some,
            samples,
            range_tiles,
            bands,
            turned.at[pl.ds(row * BLK, size * BLK)],
            outs[done : done + len(some)],
        )
        done, row = done + len(some), row + size


def next_range(steps, after, samples, range_tiles, bands):
    pulses = samples.shape[1]
    count = sum(map(len, steps))
    size = count * (GROUP // BLK) + len(steps)
    return call(
        functools.partial(next_range_body, steps),
        "next_range",
        (bf16(GROUP, 2 * pulses),) * count,
        [VMEM()] * 4,
        (VMEM(),) * count,
        [pltpu.VMEM((size * BLK, 2 * pulses), jnp.bfloat16)],
    )(after, samples, range_tiles, bands)


def own_range_body(after, samples, range_tiles, bands, az_taps, out, az_out, turned):
    group_sends([0], samples, range_tiles, bands, turned, [out])
    toeplitz_tiles(az_taps, AZ_TILES, 0, az_out)


def own_range(after, samples, range_tiles, bands, azimuth_ref):
    pulses = samples.shape[1]
    return call(
        own_range_body,
        "own_range",
        (bf16(GROUP, 2 * pulses), bf16(AZ_TILES, WIDE, WIDE)),
        [VMEM()] * 5,
        (VMEM(),) * 2,
        [pltpu.VMEM((3 * BLK, 2 * pulses), jnp.bfloat16)],
    )(after, samples, range_tiles, bands, azimuth_ref)


def gate_body(*refs):
    pass


def gate(values, after=(), flops=0):
    whole = pl.BlockSpec(memory_space=pl.ANY)
    values = list(values)
    return pl.pallas_call(
        gate_body,
        out_shape=tuple(jax.ShapeDtypeStruct(value.shape, value.dtype) for value in values),
        in_specs=[whole] * (len(values) + len(after)),
        out_specs=(whole,) * len(values),
        input_output_aliases={i: i for i in range(len(values))},
        compiler_params=pltpu.CompilerParams(vmem_limit_bytes=LIMIT),
        cost_estimate=pl.CostEstimate(flops=flops, bytes_accessed=0, transcendentals=0),
        name="gate",
    )(*values, *after)


def whole_body(count, echoes, near, far, range_tiles, bands, az_taps, out, az_out, samples, turned):
    assemble(echoes, near, far, samples)
    for block in range(count + 1):
        turned[block * BLK : (block + 1) * BLK, :] = compress(samples, range_tiles, block)
    for block in range(count):
        out[block * BLK : (block + 1) * BLK, :] = migrate(bands, turned, 0, block)
    toeplitz_tiles(az_taps, AZ_TILES, 0, az_out)


def whole_quarter(echoes, near, far, range_tiles, bands, azimuth_ref):
    pulses = echoes.shape[1]
    count = bands.shape[0] // BLK
    return call(
        functools.partial(whole_body, count),
        "whole_quarter",
        (bf16(count * BLK, 2 * pulses), bf16(AZ_TILES, WIDE, WIDE)),
        [VMEM()] * 6,
        (VMEM(),) * 2,
        [
            pltpu.VMEM((1 + count + HEAD, pulses, WIDE), jnp.bfloat16),
            pltpu.VMEM(((count + 1) * BLK, 2 * pulses), jnp.bfloat16),
        ],
    )(echoes, near, far, range_tiles, bands, azimuth_ref)


def focus_azimuth_body(steps, count, az_tiles, *rest):
    parts, out, rows, image, sems = rest[:-4], rest[-4], rest[-3], rest[-2], rest[-1]
    bins = image.shape[2]
    reach = AZ_TILES // 2
    me = lax.axis_index("pulse")
    if steps:
        for part, step in zip(parts, steps):
            rows[pl.ds(pl.multiple_of((me ^ step) * bins, bins), bins)] = part[...]
    else:
        rows[...] = parts[0][...]
    for block in range(count):
        low, high = max(0, reach - block), min(AZ_TILES, count + reach - block)
        window = jnp.concatenate(
            [
                rows[(block + tile - reach) * bins : (block + tile - reach + 1) * bins]
                for tile in range(low, high)
            ],
            axis=1,
        )
        total = jnp.dot(
            window,
            az_tiles[low:high].reshape((high - low) * WIDE, WIDE),
            preferred_element_type=jnp.float32,
        )
        span = pl.ds(block * BLK, BLK)
        for part in range(2):
            image[part, 0, :, span] = total[:, part * BLK : (part + 1) * BLK]
        pltpu.make_async_copy(
            image.at[:, :, :, span], out.at[:, :, :, span], sems.at[block]
        ).start()
    for block in range(count):
        span = pl.ds(block * BLK, BLK)
        pltpu.make_async_copy(
            image.at[:, :, :, span], out.at[:, :, :, span], sems.at[block]
        ).wait()


def focus_azimuth(steps, bins, az_tiles, parts):
    count = lax.axis_size("pulse")
    shape = (2, 1, bins, count * BLK)
    return call(
        functools.partial(focus_azimuth_body, steps, count),
        "focus_azimuth",
        jax.ShapeDtypeStruct(shape, jnp.float32),
        [VMEM()] * (1 + len(parts)),
        HBM(),
        [
            pltpu.VMEM((count * bins, WIDE), jnp.bfloat16),
            pltpu.VMEM(shape, jnp.float32),
            pltpu.SemaphoreType.DMA((count,)),
        ],
    )(az_tiles, *parts)


def per_device(echoes, range_ref, band_weights, band_offsets, azimuth_ref):
    quarter_len = echoes.shape[2]
    peers = lax.axis_size("pulse")
    quarters = lax.axis_size("rng")
    bins = quarter_len // peers
    near, far = pack(echoes)

    def swaps(start):
        pairs = [(i, i + 1) for i in range(start, quarters - 1, 2)]
        return pairs + [(j, i) for i, j in pairs]

    far = lax.ppermute(far, "rng", swaps(1))
    near = lax.ppermute(near, "rng", swaps(0))
    range_tiles, bands = prepare(range_ref, band_weights, band_offsets)

    if bins != GROUP or peers != 8:
        mine, az_tiles = whole_quarter(echoes, near, far, range_tiles, bands, azimuth_ref)
        swapped = lax.all_to_all(
            mine.reshape(peers, bins, WIDE), "pulse", split_axis=0, concat_axis=0, tiled=True
        )
        return focus_azimuth(None, bins, az_tiles, [swapped.reshape(mine.shape)])

    def send(piece, k):
        return lax.ppermute(piece, "pulse", [(i, i ^ k) for i in range(peers)])

    samples, made = first_range([4, 5], echoes, near, far, range_tiles, bands)
    parts = {4: send(made[0], 4), 5: send(made[1], 5)}
    made = next_range([[6, 7], [1]], made[0], samples, range_tiles, bands)
    parts.update({k: send(piece, k) for k, piece in zip((6, 7, 1), made)})
    made = next_range([[2, 3]], made[0], samples, range_tiles, bands)
    made = gate(made, (parts[4], parts[5]))
    parts.update({k: send(piece, k) for k, piece in zip((2, 3), made)})
    parts[0], az_tiles = own_range(made[0], samples, range_tiles, bands, azimuth_ref)
    return focus_azimuth(list(parts), bins, az_tiles, list(parts.values()))


def solution(mesh):
    return jax.shard_map(
        per_device,
        mesh=mesh,
        in_specs=(P(None, "pulse", "rng"), P(), P(None, "rng"), P("rng"), P()),
        out_specs=P(None, "rng", "pulse", None),
        check_vma=False,
    )
```

```python
import functools

import jax
import jax.numpy as jnp
from jax import lax
from jax.experimental import pallas as pl
from jax.experimental.pallas import tpu as pltpu
from jax.sharding import PartitionSpec as P

RT = 1024
AT = 512
BAND = 64
BLK = 128
HALF = BLK // 2
WIDE = 2 * BLK
RANGE_TILES = RT // BLK + 2
AZ_TILES = AT // BLK + 1
HEAD = RT // BLK + 1
GROUP = 2 * BLK
LIMIT = 24 * 1024 * 1024
PACK_FLOPS = 2 * 10**9

VMEM = functools.partial(pl.BlockSpec, memory_space=pltpu.VMEM)
HBM = functools.partial(pl.BlockSpec, memory_space=pltpu.HBM)


def call(body, name, out_shape, in_specs, out_specs, scratch_shapes=(), flops=0):
    return pl.pallas_call(
        body,
        out_shape=out_shape,
        in_specs=in_specs,
        out_specs=out_specs,
        scratch_shapes=scratch_shapes,
        compiler_params=pltpu.CompilerParams(vmem_limit_bytes=LIMIT),
        cost_estimate=pl.CostEstimate(flops=flops, bytes_accessed=0, transcendentals=0),
        name=name,
    )


def bf16(*shape):
    return jax.ShapeDtypeStruct(shape, jnp.bfloat16)


def pack_body(echoes, near, down, up):
    odd = lax.axis_index("rng") % 2 == 1

    def fill(first, last):
        for part in range(2):
            lanes = slice(part * BLK, (part + 1) * BLK)
            for block in range(HEAD):
                first[block, :, lanes] = echoes[part, :, block * BLK : (block + 1) * BLK]
            last[0, :, lanes] = echoes[part, :, echoes.shape[2] - BLK :]

    pl.when(odd)(lambda: fill(near, up))
    pl.when(jnp.logical_not(odd))(lambda: fill(down, near))


def pack(echoes):
    pulses = echoes.shape[1]
    return call(
        pack_body,
        "pack",
        (bf16(HEAD, pulses, WIDE),) * 2 + (bf16(1, pulses, WIDE),),
        [VMEM()],
        (VMEM(),) * 3,
        flops=PACK_FLOPS,
    )(echoes)


def toeplitz_tiles(taps, tiles, shift, out):
    width = (tiles + 1) * BLK
    tap_total = taps.shape[1]
    skewed = []
    for part in range(2):
        row = jnp.concatenate(
            [
                jnp.zeros((1, BLK), jnp.float32),
                taps[part : part + 1, :].astype(jnp.float32),
                jnp.zeros((1, width - BLK - tap_total), jnp.float32),
            ],
            axis=1,
        )
        row = jnp.broadcast_to(row, (BLK, width))
        skewed.append(pltpu.roll(row, shift, 1, stride=1, stride_axis=0))
    for tile in range(tiles):
        span = slice((tile + 1) * BLK, (tile + 2) * BLK)
        real = skewed[0][:, span].T
        imag = skewed[1][:, span].T
        out[tile, :BLK, :BLK] = real.astype(jnp.bfloat16)
        out[tile, :BLK, BLK:] = (-imag).astype(jnp.bfloat16)
        out[tile, BLK:, :BLK] = imag.astype(jnp.bfloat16)
        out[tile, BLK:, BLK:] = real.astype(jnp.bfloat16)


def prepare_body(range_ref, range_out):
    toeplitz_tiles(range_ref, RANGE_TILES, HALF, range_out)


def prepare(range_ref):
    return call(
        prepare_body, "prepare", bf16(RANGE_TILES, WIDE, WIDE), [VMEM()], VMEM()
    )(range_ref)


def band(weights, offsets, block):
    span = pl.ds(pl.multiple_of(block * BLK, BLK), BLK)
    placed = jnp.concatenate(
        [weights[:, span].astype(jnp.float32), jnp.zeros((BLK - BAND, BLK), jnp.float32)], axis=0
    )
    shifts = offsets[pl.ds(block, 1), :]
    for bit in range((BAND // 2).bit_length()):
        chosen = jnp.broadcast_to((shifts >> bit) & 1, (BLK, BLK)) == 1
        placed = jnp.where(chosen, pltpu.roll(placed, 1 << bit, 0), placed)
    wide = jnp.concatenate([placed.T, jnp.zeros((BLK, BLK), jnp.float32)], axis=1)
    skewed = pltpu.roll(wide, BAND // 2, 1, stride=1, stride_axis=0)
    outside = (lax.axis_index("rng") == 0) & (block == 0)
    lane = lax.broadcasted_iota(jnp.int32, (BLK, WIDE), 1)
    return jnp.where(outside & (lane < HALF), 0.0, skewed).astype(jnp.bfloat16)


def assemble(echoes, near, down, up, out):
    blocks = echoes.shape[2] // BLK
    for block in range(blocks):
        for part in range(2):
            out[block + 1, :, part * BLK : (part + 1) * BLK] = echoes[
                part, :, block * BLK : (block + 1) * BLK
            ]

    def ends(low, high):
        out[0] = low[0]
        out[blocks + 1 :] = high[...]

    odd = lax.axis_index("rng") % 2 == 1
    pl.when(odd)(lambda: ends(near, down))
    pl.when(jnp.logical_not(odd))(lambda: ends(up, near))


def compress(samples, range_tiles, block):
    window = jnp.concatenate([samples[block + tile] for tile in range(RANGE_TILES)], axis=1)
    total = jnp.dot(
        window,
        range_tiles[...].reshape(RANGE_TILES * WIDE, WIDE),
        preferred_element_type=jnp.float32,
    ).astype(jnp.bfloat16)
    return jnp.concatenate([total[:, :BLK].T, total[:, BLK:].T], axis=1)


def migrate(weights, offsets, turned, first, place):
    reach = pl.multiple_of(place * BLK, BLK)
    return jnp.dot(
        band(weights, offsets, first + place),
        turned[pl.ds(reach, WIDE)],
        preferred_element_type=jnp.float32,
    ).astype(jnp.bfloat16)


def groups_of(first, count, spots, samples, range_tiles, weights, offsets, turned, outs):
    for block in range(count + 1):
        turned[block * BLK : (block + 1) * BLK, :] = compress(samples, range_tiles, first + block)
    rows = [out.at[pl.ds(i, GROUP)] for out in outs for i in range(0, out.shape[0], GROUP)]
    for spot, out in zip(spots, rows):
        for block in range(GROUP // BLK):
            out[block * BLK : (block + 1) * BLK, :] = migrate(
                weights, offsets, turned, first, spot * (GROUP // BLK) + block
            )


def group_sends(steps, samples, range_tiles, weights, offsets, turned, outs):
    me = lax.axis_index("pulse")
    blocks = GROUP // BLK
    if len(steps) == 1:
        first, spots = blocks * (me ^ steps[0]), [0]
    else:
        first, spots = 2 * blocks * (me // 2 ^ steps[0] // 2), [me % 2 ^ k % 2 for k in steps]
    groups_of(first, blocks * len(steps), spots, samples, range_tiles, weights, offsets, turned, outs)


def first_range_body(steps, echoes, near, down, up, range_tiles, weights, offsets, samples, *rest):
    assemble(echoes, near, down, up, samples)
    group_sends(steps, samples, range_tiles, weights, offsets, rest[-1], rest[:-1])


def first_range(steps, echoes, near, down, up, range_tiles, weights, offsets):
    pulses = echoes.shape[1]
    blocks = 1 + echoes.shape[2] // BLK + HEAD
    samples, *made = call(
        functools.partial(first_range_body, steps),
        "first_range",
        (bf16(blocks, pulses, WIDE),) + (bf16(GROUP, 2 * pulses),) * len(steps),
        [VMEM()] * 7,
        (VMEM(),) * (1 + len(steps)),
        [pltpu.VMEM((5 * BLK, 2 * pulses), jnp.bfloat16)],
    )(echoes, near, down, up, range_tiles, weights, offsets)
    return samples, made


def next_range_body(steps, after, samples, range_tiles, weights, offsets, *rest):
    *outs, turned = rest
    done = row = 0
    for some in steps:
        size = len(some) * (GROUP // BLK) + 1
        group_sends(
            some,
            samples,
            range_tiles,
            weights,
            offsets,
            turned.at[pl.ds(row * BLK, size * BLK)],
            outs[done : done + len(some)],
        )
        done, row = done + len(some), row + size


def next_range(steps, after, samples, range_tiles, weights, offsets):
    pulses = samples.shape[1]
    count = sum(map(len, steps))
    size = count * (GROUP // BLK) + len(steps)
    return call(
        functools.partial(next_range_body, steps),
        "next_range",
        (bf16(GROUP, 2 * pulses),) * count,
        [VMEM()] * 5,
        (VMEM(),) * count,
        [pltpu.VMEM((size * BLK, 2 * pulses), jnp.bfloat16)],
    )(after, samples, range_tiles, weights, offsets)


def own_range_body(after, samples, range_tiles, weights, offsets, az_taps, out, az_out, turned):
    group_sends([0], samples, range_tiles, weights, offsets, turned, [out])
    toeplitz_tiles(az_taps, AZ_TILES, 0, az_out)


def own_range(after, samples, range_tiles, weights, offsets, azimuth_ref):
    pulses = samples.shape[1]
    return call(
        own_range_body,
        "own_range",
        (bf16(GROUP, 2 * pulses), bf16(AZ_TILES, WIDE, WIDE)),
        [VMEM()] * 6,
        (VMEM(),) * 2,
        [pltpu.VMEM((3 * BLK, 2 * pulses), jnp.bfloat16)],
    )(after, samples, range_tiles, weights, offsets, azimuth_ref)


def gate_body(*refs):
    pass


def gate(values, after=(), flops=0):
    whole = pl.BlockSpec(memory_space=pl.ANY)
    values = list(values)
    return pl.pallas_call(
        gate_body,
        out_shape=tuple(jax.ShapeDtypeStruct(value.shape, value.dtype) for value in values),
        in_specs=[whole] * (len(values) + len(after)),
        out_specs=(whole,) * len(values),
        input_output_aliases={i: i for i in range(len(values))},
        compiler_params=pltpu.CompilerParams(vmem_limit_bytes=LIMIT),
        cost_estimate=pl.CostEstimate(flops=flops, bytes_accessed=0, transcendentals=0),
        name="gate",
    )(*values, *after)


def whole_body(count, echoes, near, down, up, range_tiles, weights, offsets, az_taps, out, az_out, samples, turned):
    assemble(echoes, near, down, up, samples)
    for block in range(count + 1):
        turned[block * BLK : (block + 1) * BLK, :] = compress(samples, range_tiles, block)
    for block in range(count):
        out[block * BLK : (block + 1) * BLK, :] = migrate(weights, offsets, turned, 0, block)
    toeplitz_tiles(az_taps, AZ_TILES, 0, az_out)


def whole_quarter(echoes, near, down, up, range_tiles, weights, offsets, azimuth_ref):
    pulses = echoes.shape[1]
    count = weights.shape[1] // BLK
    return call(
        functools.partial(whole_body, count),
        "whole_quarter",
        (bf16(count * BLK, 2 * pulses), bf16(AZ_TILES, WIDE, WIDE)),
        [VMEM()] * 8,
        (VMEM(),) * 2,
        [
            pltpu.VMEM((1 + count + HEAD, pulses, WIDE), jnp.bfloat16),
            pltpu.VMEM(((count + 1) * BLK, 2 * pulses), jnp.bfloat16),
        ],
    )(echoes, near, down, up, range_tiles, weights, offsets, azimuth_ref)


def azimuth_rows(bins, steps, parts, rows):
    me = lax.axis_index("pulse")
    for part, step in zip(parts, steps):
        rows[pl.ds(pl.multiple_of((me ^ step) * bins, bins), bins)] = part[...]


def azimuth_blocks(bins, count, rows, az_tiles, image, done=lambda block: None):
    reach = AZ_TILES // 2
    for block in range(count):
        low, high = max(0, reach - block), min(AZ_TILES, count + reach - block)
        window = jnp.concatenate(
            [
                rows[(block + tile - reach) * bins : (block + tile - reach + 1) * bins]
                for tile in range(low, high)
            ],
            axis=1,
        )
        total = jnp.dot(
            window,
            az_tiles[low:high].reshape((high - low) * WIDE, WIDE),
            preferred_element_type=jnp.float32,
        )
        for part in range(2):
            image[part, 0, :, block * BLK : (block + 1) * BLK] = total[
                :, part * BLK : (part + 1) * BLK
            ]
        done(block)


def column(image, out, sems, block):
    span = pl.ds(pl.multiple_of(block * BLK, BLK), BLK)
    return pltpu.make_async_copy(image.at[:, :, :, span], out.at[:, :, :, span], sems.at[block])


def azimuth_body(steps, az_tiles, *rest):
    *parts, out, rows, image, sems = rest
    bins = image.shape[2]
    count = image.shape[3] // BLK
    if steps:
        azimuth_rows(bins, steps, parts, rows)
    else:
        rows[...] = parts[0][...]
    azimuth_blocks(
        bins,
        count,
        rows,
        az_tiles,
        image,
        lambda block: column(image, out, sems, block).start(),
    )
    for block in range(count):
        column(image, out, sems, block).wait()


def azimuth(steps, count, az_tiles, parts):
    bins = sum(part.shape[0] for part in parts) // count
    shape = (2, 1, bins, count * BLK)
    return call(
        functools.partial(azimuth_body, steps),
        "azimuth",
        jax.ShapeDtypeStruct(shape, jnp.float32),
        [VMEM()] * (1 + len(parts)),
        HBM(),
        [
            pltpu.VMEM((count * bins, WIDE), jnp.bfloat16),
            pltpu.VMEM(shape, jnp.float32),
            pltpu.SemaphoreType.DMA((count,)),
        ],
    )(az_tiles, *parts)


def per_device(echoes, range_ref, band_weights, band_offsets, azimuth_ref):
    quarter_len = echoes.shape[2]
    peers = lax.axis_size("pulse")
    quarters = lax.axis_size("rng")
    bins = quarter_len // peers
    near, down, up = pack(echoes)
    cores = [(i, i + 1) for i in range(0, quarters - 1, 2)]
    chips = [(i, i + 1) for i in range(1, quarters - 1, 2)]
    near = lax.ppermute(near, "rng", cores + [(j, i) for i, j in cores])
    down = lax.ppermute(down, "rng", [(j, i) for i, j in chips])
    up = lax.ppermute(up, "rng", chips)
    range_tiles = prepare(range_ref)
    weights, offsets = band_weights, band_offsets.reshape(-1, BLK)

    if bins != GROUP or peers != 8:
        mine, az_tiles = whole_quarter(echoes, near, down, up, range_tiles, weights, offsets, azimuth_ref)
        swapped = lax.all_to_all(
            mine.reshape(peers, bins, WIDE), "pulse", split_axis=0, concat_axis=0, tiled=True
        )
        return azimuth(None, peers, az_tiles, [swapped.reshape(mine.shape)])

    def send(piece, k):
        return lax.ppermute(piece, "pulse", [(i, i ^ k) for i in range(peers)])

    samples, made = first_range([4, 5], echoes, near, down, up, range_tiles, weights, offsets)
    parts = {k: send(piece, k) for k, piece in zip([4, 5], made)}
    for some in [[6, 7]]:
        made = next_range([some], made[0], samples, range_tiles, weights, offsets)
        parts.update({k: send(piece, k) for k, piece in zip(some, made)})
    ready = {}
    for some in [[2, 3], [1]]:
        made = next_range([some], made[0], samples, range_tiles, weights, offsets)
        ready.update(zip(some, made))
    parts[3] = send(ready[3], 3)
    parts[1] = send(gate([ready[1]], (parts[5],))[0], 1)
    parts[2] = send(gate([ready[2]], (parts[4],))[0], 2)
    parts[0], az_tiles = own_range(made[0], samples, range_tiles, weights, offsets, azimuth_ref)
    held = gate((parts[6], parts[7]), (), 1000000000) + (parts[3],)
    parts.update(zip((6, 7, 3), gate(held, (), 2 * 10**8)))
    return azimuth(list(parts), peers, az_tiles, list(parts.values()))


def solution(mesh):
    return jax.shard_map(
        per_device,
        mesh=mesh,
        in_specs=(P(None, "pulse", "rng"), P(), P(None, "rng"), P("rng"), P()),
        out_specs=P(None, "rng", "pulse", None),
        check_vma=False,
    )
```

```python
import functools

import jax
import jax.numpy as jnp
from jax import lax
from jax.experimental import pallas as pl
from jax.experimental.pallas import tpu as pltpu
from jax.sharding import PartitionSpec as P

RT = 1024
AT = 512
BAND = 64
BLK = 128
HALF = BLK // 2
WIDE = 2 * BLK
RANGE_TILES = RT // BLK + 2
AZ_TILES = AT // BLK + 1
HEAD = RT // BLK + 1
GROUP = 2 * BLK
LIMIT = 24 * 1024 * 1024
PACK_FLOPS = 2 * 10**9

VMEM = functools.partial(pl.BlockSpec, memory_space=pltpu.VMEM)
HBM = functools.partial(pl.BlockSpec, memory_space=pltpu.HBM)


def call(body, name, out_shape, in_specs, out_specs, scratch_shapes=(), flops=0):
    return pl.pallas_call(
        body,
        out_shape=out_shape,
        in_specs=in_specs,
        out_specs=out_specs,
        scratch_shapes=scratch_shapes,
        compiler_params=pltpu.CompilerParams(vmem_limit_bytes=LIMIT),
        cost_estimate=pl.CostEstimate(flops=flops, bytes_accessed=0, transcendentals=0),
        name=name,
    )


def bf16(*shape):
    return jax.ShapeDtypeStruct(shape, jnp.bfloat16)


def pack_body(echoes, near, down, up):
    odd = lax.axis_index("rng") % 2 == 1

    def fill(first, last):
        for part in range(2):
            lanes = slice(part * BLK, (part + 1) * BLK)
            for block in range(HEAD):
                first[block, :, lanes] = echoes[part, :, block * BLK : (block + 1) * BLK]
            last[0, :, lanes] = echoes[part, :, echoes.shape[2] - BLK :]

    pl.when(odd)(lambda: fill(near, up))
    pl.when(jnp.logical_not(odd))(lambda: fill(down, near))


def pack(echoes):
    pulses = echoes.shape[1]
    return call(
        pack_body,
        "pack",
        (bf16(HEAD, pulses, WIDE),) * 2 + (bf16(1, pulses, WIDE),),
        [VMEM()],
        (VMEM(),) * 3,
        flops=PACK_FLOPS,
    )(echoes)


def toeplitz_tiles(taps, tiles, shift, out):
    width = (tiles + 1) * BLK
    tap_total = taps.shape[1]
    skewed = []
    for part in range(2):
        row = jnp.concatenate(
            [
                jnp.zeros((1, BLK), jnp.float32),
                taps[part : part + 1, :].astype(jnp.float32),
                jnp.zeros((1, width - BLK - tap_total), jnp.float32),
            ],
            axis=1,
        )
        row = jnp.broadcast_to(row, (BLK, width))
        skewed.append(pltpu.roll(row, shift, 1, stride=1, stride_axis=0))
    for tile in range(tiles):
        span = slice((tile + 1) * BLK, (tile + 2) * BLK)
        real = skewed[0][:, span].T
        imag = skewed[1][:, span].T
        out[tile, :BLK, :BLK] = real.astype(jnp.bfloat16)
        out[tile, :BLK, BLK:] = (-imag).astype(jnp.bfloat16)
        out[tile, BLK:, :BLK] = imag.astype(jnp.bfloat16)
        out[tile, BLK:, BLK:] = real.astype(jnp.bfloat16)


def band(weights, offsets, block):
    span = pl.ds(pl.multiple_of(block * BLK, BLK), BLK)
    placed = jnp.concatenate(
        [weights[:, span].astype(jnp.float32), jnp.zeros((BLK - BAND, BLK), jnp.float32)], axis=0
    )
    shifts = offsets[pl.ds(block, 1), :]
    for bit in range((BAND // 2).bit_length()):
        chosen = jnp.broadcast_to((shifts >> bit) & 1, (BLK, BLK)) == 1
        placed = jnp.where(chosen, pltpu.roll(placed, 1 << bit, 0), placed)
    wide = jnp.concatenate([placed.T, jnp.zeros((BLK, BLK), jnp.float32)], axis=1)
    skewed = pltpu.roll(wide, BAND // 2, 1, stride=1, stride_axis=0)
    outside = (lax.axis_index("rng") == 0) & (block == 0)
    lane = lax.broadcasted_iota(jnp.int32, (BLK, WIDE), 1)
    return jnp.where(outside & (lane < HALF), 0.0, skewed).astype(jnp.bfloat16)


def prepare_body(echoes, range_ref, samples, range_out):
    toeplitz_tiles(range_ref, RANGE_TILES, HALF, range_out)
    for block in range(echoes.shape[2] // BLK):
        for part in range(2):
            samples[block + 1, :, part * BLK : (part + 1) * BLK] = echoes[
                part, :, block * BLK : (block + 1) * BLK
            ]


def prepare(echoes, range_ref):
    blocks = 1 + echoes.shape[2] // BLK + HEAD
    return call(
        prepare_body,
        "prepare",
        (bf16(blocks, echoes.shape[1], WIDE), bf16(RANGE_TILES, WIDE, WIDE)),
        [VMEM()] * 2,
        (VMEM(),) * 2,
    )(echoes, range_ref)


def add_ends(near, down, up, out):
    count = near.shape[0]

    def ends(low, high):
        out[0] = low[0]
        out[out.shape[0] - count :] = high[...]

    odd = lax.axis_index("rng") % 2 == 1
    pl.when(odd)(lambda: ends(near, down))
    pl.when(jnp.logical_not(odd))(lambda: ends(up, near))


def compress(samples, range_tiles, block):
    window = jnp.concatenate([samples[block + tile] for tile in range(RANGE_TILES)], axis=1)
    total = jnp.dot(
        window,
        range_tiles[...].reshape(RANGE_TILES * WIDE, WIDE),
        preferred_element_type=jnp.float32,
    ).astype(jnp.bfloat16)
    return jnp.concatenate([total[:, :BLK].T, total[:, BLK:].T], axis=1)


def migrate(weights, offsets, turned, first, place):
    reach = pl.multiple_of(place * BLK, BLK)
    return jnp.dot(
        band(weights, offsets, first + place),
        turned[pl.ds(reach, WIDE)],
        preferred_element_type=jnp.float32,
    ).astype(jnp.bfloat16)


def group_sends(steps, samples, range_tiles, weights, offsets, turned, outs):
    me = lax.axis_index("pulse")
    blocks = GROUP // BLK
    if len(steps) == 1:
        first, spots = blocks * (me ^ steps[0]), [0]
    else:
        first, spots = 2 * blocks * (me // 2 ^ steps[0] // 2), [me % 2 ^ k % 2 for k in steps]
    for block in range(blocks * len(steps) + 1):
        turned[block * BLK : (block + 1) * BLK, :] = compress(samples, range_tiles, first + block)
    for spot, out in zip(spots, outs):
        for block in range(blocks):
            out[block * BLK : (block + 1) * BLK, :] = migrate(
                weights, offsets, turned, first, spot * blocks + block
            )


def first_range_body(
    steps, start, near, down, up, range_tiles, weights, offsets, samples, *rest
):
    add_ends(near, down, up, samples)
    group_sends(steps, samples, range_tiles, weights, offsets, rest[-1], rest[:-1])


def first_range(steps, samples, near, down, up, range_tiles, weights, offsets):
    pulses = samples.shape[1]
    samples, *made = pl.pallas_call(
        functools.partial(first_range_body, steps),
        out_shape=(jax.ShapeDtypeStruct(samples.shape, samples.dtype),)
        + (bf16(GROUP, 2 * pulses),) * len(steps),
        in_specs=[VMEM()] * 7,
        out_specs=(VMEM(),) * (1 + len(steps)),
        scratch_shapes=[pltpu.VMEM((5 * BLK, 2 * pulses), jnp.bfloat16)],
        input_output_aliases={0: 0},
        compiler_params=pltpu.CompilerParams(vmem_limit_bytes=LIMIT),
        cost_estimate=pl.CostEstimate(flops=0, bytes_accessed=0, transcendentals=0),
        name="first_range",
    )(samples, near, down, up, range_tiles, weights, offsets)
    return samples, made


def next_range_body(steps, after, samples, range_tiles, weights, offsets, *rest):
    *outs, turned = rest
    done = row = 0
    for some in steps:
        size = len(some) * (GROUP // BLK) + 1
        group_sends(
            some,
            samples,
            range_tiles,
            weights,
            offsets,
            turned.at[pl.ds(row * BLK, size * BLK)],
            outs[done : done + len(some)],
        )
        done, row = done + len(some), row + size


def next_range(steps, after, samples, range_tiles, weights, offsets):
    pulses = samples.shape[1]
    count = sum(map(len, steps))
    size = count * (GROUP // BLK) + len(steps)
    return call(
        functools.partial(next_range_body, steps),
        "next_range",
        (bf16(GROUP, 2 * pulses),) * count,
        [VMEM()] * 5,
        (VMEM(),) * count,
        [pltpu.VMEM((size * BLK, 2 * pulses), jnp.bfloat16)],
    )(after, samples, range_tiles, weights, offsets)


def own_range_body(after, samples, range_tiles, weights, offsets, az_taps, out, az_out, turned):
    group_sends([0], samples, range_tiles, weights, offsets, turned, [out])
    toeplitz_tiles(az_taps, AZ_TILES, 0, az_out)


def own_range(after, samples, range_tiles, weights, offsets, azimuth_ref):
    pulses = samples.shape[1]
    return call(
        own_range_body,
        "own_range",
        (bf16(GROUP, 2 * pulses), bf16(AZ_TILES, WIDE, WIDE)),
        [VMEM()] * 6,
        (VMEM(),) * 2,
        [pltpu.VMEM((3 * BLK, 2 * pulses), jnp.bfloat16)],
    )(after, samples, range_tiles, weights, offsets, azimuth_ref)


def gate_body(*refs):
    pass


def gate(values, after=(), flops=0):
    whole = pl.BlockSpec(memory_space=pl.ANY)
    values = list(values)
    return pl.pallas_call(
        gate_body,
        out_shape=tuple(jax.ShapeDtypeStruct(value.shape, value.dtype) for value in values),
        in_specs=[whole] * (len(values) + len(after)),
        out_specs=(whole,) * len(values),
        input_output_aliases={i: i for i in range(len(values))},
        compiler_params=pltpu.CompilerParams(vmem_limit_bytes=LIMIT),
        cost_estimate=pl.CostEstimate(flops=flops, bytes_accessed=0, transcendentals=0),
        name="gate",
    )(*values, *after)


def whole_body(count, start, near, down, up, range_tiles, weights, offsets, az_taps, *rest):
    out, az_out, samples, turned = rest
    samples[...] = start[...]
    add_ends(near, down, up, samples)
    for block in range(count + 1):
        turned[block * BLK : (block + 1) * BLK, :] = compress(samples, range_tiles, block)
    for block in range(count):
        out[block * BLK : (block + 1) * BLK, :] = migrate(weights, offsets, turned, 0, block)
    toeplitz_tiles(az_taps, AZ_TILES, 0, az_out)


def whole_quarter(samples, near, down, up, range_tiles, weights, offsets, azimuth_ref):
    pulses = samples.shape[1]
    count = weights.shape[1] // BLK
    return call(
        functools.partial(whole_body, count),
        "whole_quarter",
        (bf16(count * BLK, 2 * pulses), bf16(AZ_TILES, WIDE, WIDE)),
        [VMEM()] * 8,
        (VMEM(),) * 2,
        [
            pltpu.VMEM(samples.shape, jnp.bfloat16),
            pltpu.VMEM(((count + 1) * BLK, 2 * pulses), jnp.bfloat16),
        ],
    )(samples, near, down, up, range_tiles, weights, offsets, azimuth_ref)


def azimuth_rows(bins, steps, parts, rows):
    me = lax.axis_index("pulse")
    for part, step in zip(parts, steps):
        rows[pl.ds(pl.multiple_of((me ^ step) * bins, bins), bins)] = part[...]


def azimuth_blocks(bins, count, rows, az_tiles, image, done=lambda block: None):
    reach = AZ_TILES // 2
    for block in range(count):
        low, high = max(0, reach - block), min(AZ_TILES, count + reach - block)
        window = jnp.concatenate(
            [
                rows[(block + tile - reach) * bins : (block + tile - reach + 1) * bins]
                for tile in range(low, high)
            ],
            axis=1,
        )
        total = jnp.dot(
            window,
            az_tiles[low:high].reshape((high - low) * WIDE, WIDE),
            preferred_element_type=jnp.float32,
        )
        for part in range(2):
            image[part, 0, :, block * BLK : (block + 1) * BLK] = total[
                :, part * BLK : (part + 1) * BLK
            ]
        done(block)


def column(image, out, sems, block):
    span = pl.ds(pl.multiple_of(block * BLK, BLK), BLK)
    return pltpu.make_async_copy(image.at[:, :, :, span], out.at[:, :, :, span], sems.at[block])


def azimuth_body(steps, az_tiles, *rest):
    *parts, out, rows, image, sems = rest
    bins = image.shape[2]
    count = image.shape[3] // BLK
    if steps:
        azimuth_rows(bins, steps, parts, rows)
    else:
        rows[...] = parts[0][...]
    azimuth_blocks(
        bins,
        count,
        rows,
        az_tiles,
        image,
        lambda block: column(image, out, sems, block).start(),
    )
    for block in range(count):
        column(image, out, sems, block).wait()


def azimuth(steps, count, az_tiles, parts):
    bins = sum(part.shape[0] for part in parts) // count
    shape = (2, 1, bins, count * BLK)
    return call(
        functools.partial(azimuth_body, steps),
        "azimuth",
        jax.ShapeDtypeStruct(shape, jnp.float32),
        [VMEM()] * (1 + len(parts)),
        HBM(),
        [
            pltpu.VMEM((count * bins, WIDE), jnp.bfloat16),
            pltpu.VMEM(shape, jnp.float32),
            pltpu.SemaphoreType.DMA((count,)),
        ],
    )(az_tiles, *parts)


def azimuth_most_body(steps, absent, az_tiles, *rest):
    *parts, image, rows = rest
    bins = image.shape[2]
    azimuth_rows(bins, [absent], [jnp.zeros((bins, WIDE), jnp.bfloat16)], rows)
    azimuth_rows(bins, steps, parts, rows)
    azimuth_blocks(bins, image.shape[3] // BLK, rows, az_tiles, image)


def azimuth_most(steps, absent, az_tiles, parts):
    bins = parts[0].shape[0]
    count = len(steps) + 1
    return call(
        functools.partial(azimuth_most_body, steps, absent),
        "azimuth_most",
        jax.ShapeDtypeStruct((2, 1, bins, count * BLK), jnp.float32),
        [VMEM()] * (1 + len(parts)),
        VMEM(),
        [pltpu.VMEM((count * bins, WIDE), jnp.bfloat16)],
    )(az_tiles, *parts)


def azimuth_last_body(step, az_tiles, most, part, out, image, sems):
    count = most.shape[3] // BLK
    low = (lax.axis_index("pulse") ^ step) - AZ_TILES // 2

    def move(source, place, block):
        span = pl.ds(pl.multiple_of(block * BLK, BLK), BLK)
        return pltpu.make_async_copy(
            source.at[:, :, :, pl.ds(pl.multiple_of(place * BLK, BLK), BLK)],
            out.at[:, :, :, span],
            sems.at[block],
        )

    for block in range(count):
        pl.when((block < low) | (block >= low + AZ_TILES))(move(most, block, block).start)
    for i in range(AZ_TILES):
        total = jnp.dot(
            part[...], az_tiles[AZ_TILES - 1 - i], preferred_element_type=jnp.float32
        )
        block = low + i
        held = pl.ds(pl.multiple_of(jnp.clip(block, 0, count - 1) * BLK, BLK), BLK)
        for side in range(2):
            image[side, 0, :, i * BLK : (i + 1) * BLK] = (
                most[side, 0, :, held] + total[:, side * BLK : (side + 1) * BLK]
            )
        inside = (block >= 0) & (block < count)
        pl.when(inside)(lambda i=i, block=block: move(image, i, block).start())
    for block in range(count):
        move(most, block, block).wait()


def azimuth_last(step, az_tiles, most, part):
    return call(
        functools.partial(azimuth_last_body, step),
        "azimuth_last",
        jax.ShapeDtypeStruct(most.shape, most.dtype),
        [VMEM()] * 3,
        HBM(),
        [
            pltpu.VMEM(most.shape[:3] + (AZ_TILES * BLK,), jnp.float32),
            pltpu.SemaphoreType.DMA((most.shape[3] // BLK,)),
        ],
    )(az_tiles, most, part)


def per_device(echoes, range_ref, band_weights, band_offsets, azimuth_ref):
    quarter_len = echoes.shape[2]
    peers = lax.axis_size("pulse")
    quarters = lax.axis_size("rng")
    bins = quarter_len // peers
    near, down, up = pack(echoes)
    cores = [(i, i + 1) for i in range(0, quarters - 1, 2)]
    chips = [(i, i + 1) for i in range(1, quarters - 1, 2)]
    near = lax.ppermute(near, "rng", cores + [(j, i) for i, j in cores])
    down = lax.ppermute(down, "rng", [(j, i) for i, j in chips])
    up = lax.ppermute(up, "rng", chips)
    weights, offsets = band_weights, band_offsets.reshape(-1, BLK)
    samples, range_tiles = prepare(echoes, range_ref)

    if bins != GROUP or peers != 8:
        mine, az_tiles = whole_quarter(
            samples, near, down, up, range_tiles, weights, offsets, azimuth_ref
        )
        swapped = lax.all_to_all(
            mine.reshape(peers, bins, WIDE), "pulse", split_axis=0, concat_axis=0, tiled=True
        )
        return azimuth(None, peers, az_tiles, [swapped.reshape(mine.shape)])

    def send(piece, k):
        return lax.ppermute(piece, "pulse", [(i, i ^ k) for i in range(peers)])

    samples, made = first_range(
        [4, 5], samples, near, down, up, range_tiles, weights, offsets
    )
    parts = {k: send(piece, k) for k, piece in zip((4, 5), made)}
    made = next_range([[6, 7]], made[0], samples, range_tiles, weights, offsets)
    parts.update({k: send(piece, k) for k, piece in zip((6, 7), made)})
    ready = {}
    for some in [[2, 3], [1]]:
        made = next_range([some], made[0], samples, range_tiles, weights, offsets)
        ready.update(zip(some, made))
    parts[3] = send(ready[3], 3)
    parts[1] = send(gate([ready[1]], (parts[5],))[0], 1)
    parts[2] = send(gate([ready[2]], (parts[4],))[0], 2)
    parts[0], az_tiles = own_range(parts[5], samples, range_tiles, weights, offsets, azimuth_ref)
    held = gate((parts[6], parts[7]), (), 1000000000) + (parts[3],)
    parts.update(zip((6, 7, 3), gate(held, (), 2 * 10**8)))
    last = parts.pop(2)
    most = azimuth_most(list(parts), 2, az_tiles, list(parts.values()))
    return azimuth_last(2, az_tiles, most, last)


def solution(mesh):
    return jax.shard_map(
        per_device,
        mesh=mesh,
        in_specs=(P(None, "pulse", "rng"), P(), P(None, "rng"), P("rng"), P()),
        out_specs=P(None, "rng", "pulse", None),
        check_vma=False,
    )
```

```python
import functools

import jax
import jax.numpy as jnp
from jax import lax
from jax.experimental import pallas as pl
from jax.experimental.pallas import tpu as pltpu
from jax.sharding import PartitionSpec as P

RT = 1024
AT = 512
BAND = 64
BLK = 128
HALF = BLK // 2
WIDE = 2 * BLK
RANGE_TILES = RT // BLK + 2
AZ_TILES = AT // BLK + 1
HEAD = RT // BLK + 1
GROUP = 2 * BLK
LIMIT = 24 * 1024 * 1024
PACK_FLOPS = 2 * 10**9

VMEM = functools.partial(pl.BlockSpec, memory_space=pltpu.VMEM)
HBM = functools.partial(pl.BlockSpec, memory_space=pltpu.HBM)


def call(body, name, out_shape, in_specs, out_specs, scratch_shapes=(), flops=0):
    return pl.pallas_call(
        body,
        out_shape=out_shape,
        in_specs=in_specs,
        out_specs=out_specs,
        scratch_shapes=scratch_shapes,
        compiler_params=pltpu.CompilerParams(vmem_limit_bytes=LIMIT),
        cost_estimate=pl.CostEstimate(flops=flops, bytes_accessed=0, transcendentals=0),
        name=name,
    )


def bf16(*shape):
    return jax.ShapeDtypeStruct(shape, jnp.bfloat16)


def pack_body(echoes, near, down, up):
    odd = lax.axis_index("rng") % 2 == 1

    def block(part, place):
        return echoes[part, :, place * BLK : (place + 1) * BLK]

    def put_last(out):
        for part in range(2):
            out[0, :, part * BLK : (part + 1) * BLK] = block(part, echoes.shape[2] // BLK - 1)

    @pl.when(odd)
    def to_even():
        for part in range(2):
            for place in range(HEAD):
                near[place, :, part * BLK : (part + 1) * BLK] = block(part, place)
        put_last(up)

    @pl.when(jnp.logical_not(odd))
    def to_odd():
        for part in range(2):
            for place in range(HEAD - 1):
                down[2 * place + part] = block(part, place)
        lane = lax.broadcasted_iota(jnp.int32, near.shape[1:2] + (BLK,), 1)
        real, imag = (block(part, HEAD - 1).astype(jnp.float32) for part in range(2))
        joined = jnp.where(lane < HALF, real, pltpu.roll(imag, HALF, 1))
        down[2 * HEAD - 2] = joined.astype(jnp.bfloat16)
        put_last(near)


def pack(echoes):
    pulses = echoes.shape[1]
    return call(
        pack_body,
        "pack",
        (
            bf16(HEAD, pulses, WIDE),
            bf16(2 * HEAD - 1, pulses, BLK),
            bf16(1, pulses, WIDE),
        ),
        [VMEM()],
        (VMEM(),) * 3,
        flops=PACK_FLOPS,
    )(echoes)


def toeplitz_tiles(taps, tiles, shift, out):
    width = (tiles + 1) * BLK
    tap_total = taps.shape[1]
    skewed = []
    for part in range(2):
        row = jnp.concatenate(
            [
                jnp.zeros((1, BLK), jnp.float32),
                taps[part : part + 1, :].astype(jnp.float32),
                jnp.zeros((1, width - BLK - tap_total), jnp.float32),
            ],
            axis=1,
        )
        row = jnp.broadcast_to(row, (BLK, width))
        skewed.append(pltpu.roll(row, shift, 1, stride=1, stride_axis=0))
    for tile in range(tiles):
        span = slice((tile + 1) * BLK, (tile + 2) * BLK)
        real = skewed[0][:, span].T
        imag = skewed[1][:, span].T
        out[tile, :BLK, :BLK] = real.astype(jnp.bfloat16)
        out[tile, :BLK, BLK:] = (-imag).astype(jnp.bfloat16)
        out[tile, BLK:, :BLK] = imag.astype(jnp.bfloat16)
        out[tile, BLK:, BLK:] = real.astype(jnp.bfloat16)


def band(weights, offsets, block):
    span = pl.ds(pl.multiple_of(block * BLK, BLK), BLK)
    placed = jnp.concatenate(
        [weights[:, span].astype(jnp.float32), jnp.zeros((BLK - BAND, BLK), jnp.float32)], axis=0
    )
    shifts = offsets[pl.ds(block, 1), :]
    for bit in range((BAND // 2).bit_length()):
        chosen = jnp.broadcast_to((shifts >> bit) & 1, (BLK, BLK)) == 1
        placed = jnp.where(chosen, pltpu.roll(placed, 1 << bit, 0), placed)
    wide = jnp.concatenate([placed.T, jnp.zeros((BLK, BLK), jnp.float32)], axis=1)
    skewed = pltpu.roll(wide, BAND // 2, 1, stride=1, stride_axis=0)
    outside = (lax.axis_index("rng") == 0) & (block == 0)
    lane = lax.broadcasted_iota(jnp.int32, (BLK, WIDE), 1)
    return jnp.where(outside & (lane < HALF), 0.0, skewed).astype(jnp.bfloat16)


def prepare_body(echoes, range_ref, samples, range_out):
    toeplitz_tiles(range_ref, RANGE_TILES, HALF, range_out)
    for block in range(echoes.shape[2] // BLK):
        for part in range(2):
            samples[block + 1, :, part * BLK : (part + 1) * BLK] = echoes[
                part, :, block * BLK : (block + 1) * BLK
            ]


def prepare(echoes, range_ref):
    blocks = 1 + echoes.shape[2] // BLK + HEAD
    return call(
        prepare_body,
        "prepare",
        (bf16(blocks, echoes.shape[1], WIDE), bf16(RANGE_TILES, WIDE, WIDE)),
        [VMEM()] * 2,
        (VMEM(),) * 2,
    )(echoes, range_ref)


def add_ends(near, down, up, out):
    start = out.shape[0] - HEAD
    odd = lax.axis_index("rng") % 2 == 1

    @pl.when(odd)
    def from_even():
        out[0] = near[0]
        for place in range(HEAD - 1):
            for part in range(2):
                out[start + place, :, part * BLK : (part + 1) * BLK] = down[2 * place + part]
        lane = lax.broadcasted_iota(jnp.int32, down.shape[1:], 1)
        joined = down[2 * HEAD - 2].astype(jnp.float32)
        for part, value in enumerate((joined, pltpu.roll(joined, HALF, 1))):
            out[start + HEAD - 1, :, part * BLK : (part + 1) * BLK] = jnp.where(
                lane < HALF, value, 0.0
            ).astype(jnp.bfloat16)

    @pl.when(jnp.logical_not(odd))
    def from_odd():
        out[0] = up[0]
        out[start:] = near[...]


def compress(samples, range_tiles, block):
    window = jnp.concatenate([samples[block + tile] for tile in range(RANGE_TILES)], axis=1)
    total = jnp.dot(
        window,
        range_tiles[...].reshape(RANGE_TILES * WIDE, WIDE),
        preferred_element_type=jnp.float32,
    ).astype(jnp.bfloat16)
    return jnp.concatenate([total[:, :BLK].T, total[:, BLK:].T], axis=1)


def migrate(weights, offsets, turned, first, place):
    reach = pl.multiple_of(place * BLK, BLK)
    return jnp.dot(
        band(weights, offsets, first + place),
        turned[pl.ds(reach, WIDE)],
        preferred_element_type=jnp.float32,
    ).astype(jnp.bfloat16)


def group_sends(steps, samples, range_tiles, weights, offsets, turned, outs):
    me = lax.axis_index("pulse")
    blocks = GROUP // BLK
    if len(steps) == 1:
        first, spots = blocks * (me ^ steps[0]), [0]
    else:
        first, spots = 2 * blocks * (me // 2 ^ steps[0] // 2), [me % 2 ^ k % 2 for k in steps]
    for block in range(blocks * len(steps) + 1):
        turned[block * BLK : (block + 1) * BLK, :] = compress(samples, range_tiles, first + block)
    for spot, out in zip(spots, outs):
        for block in range(blocks):
            out[block * BLK : (block + 1) * BLK, :] = migrate(
                weights, offsets, turned, first, spot * blocks + block
            )


def first_range_body(
    steps, start, near, down, up, range_tiles, weights, offsets, samples, *rest
):
    add_ends(near, down, up, samples)
    group_sends(steps, samples, range_tiles, weights, offsets, rest[-1], rest[:-1])


def first_range(steps, samples, near, down, up, range_tiles, weights, offsets):
    pulses = samples.shape[1]
    samples, *made = pl.pallas_call(
        functools.partial(first_range_body, steps),
        out_shape=(jax.ShapeDtypeStruct(samples.shape, samples.dtype),)
        + (bf16(GROUP, 2 * pulses),) * len(steps),
        in_specs=[VMEM()] * 7,
        out_specs=(VMEM(),) * (1 + len(steps)),
        scratch_shapes=[pltpu.VMEM((5 * BLK, 2 * pulses), jnp.bfloat16)],
        input_output_aliases={0: 0},
        compiler_params=pltpu.CompilerParams(vmem_limit_bytes=LIMIT),
        cost_estimate=pl.CostEstimate(flops=0, bytes_accessed=0, transcendentals=0),
        name="first_range",
    )(samples, near, down, up, range_tiles, weights, offsets)
    return samples, made


def next_range_body(steps, after, samples, range_tiles, weights, offsets, *rest):
    *outs, turned = rest
    done = row = 0
    for some in steps:
        size = len(some) * (GROUP // BLK) + 1
        group_sends(
            some,
            samples,
            range_tiles,
            weights,
            offsets,
            turned.at[pl.ds(row * BLK, size * BLK)],
            outs[done : done + len(some)],
        )
        done, row = done + len(some), row + size


def next_range(steps, after, samples, range_tiles, weights, offsets):
    pulses = samples.shape[1]
    count = sum(map(len, steps))
    size = count * (GROUP // BLK) + len(steps)
    return call(
        functools.partial(next_range_body, steps),
        "next_range",
        (bf16(GROUP, 2 * pulses),) * count,
        [VMEM()] * 5,
        (VMEM(),) * count,
        [pltpu.VMEM((size * BLK, 2 * pulses), jnp.bfloat16)],
    )(after, samples, range_tiles, weights, offsets)


def own_range_body(after, samples, range_tiles, weights, offsets, az_taps, out, az_out, turned):
    group_sends([0], samples, range_tiles, weights, offsets, turned, [out])
    toeplitz_tiles(az_taps, AZ_TILES, 0, az_out)


def own_range(after, samples, range_tiles, weights, offsets, azimuth_ref):
    pulses = samples.shape[1]
    return call(
        own_range_body,
        "own_range",
        (bf16(GROUP, 2 * pulses), bf16(AZ_TILES, WIDE, WIDE)),
        [VMEM()] * 6,
        (VMEM(),) * 2,
        [pltpu.VMEM((3 * BLK, 2 * pulses), jnp.bfloat16)],
    )(after, samples, range_tiles, weights, offsets, azimuth_ref)


def gate_body(*refs):
    pass


def gate(values, after=(), flops=0):
    whole = pl.BlockSpec(memory_space=pl.ANY)
    values = list(values)
    return pl.pallas_call(
        gate_body,
        out_shape=tuple(jax.ShapeDtypeStruct(value.shape, value.dtype) for value in values),
        in_specs=[whole] * (len(values) + len(after)),
        out_specs=(whole,) * len(values),
        input_output_aliases={i: i for i in range(len(values))},
        compiler_params=pltpu.CompilerParams(vmem_limit_bytes=LIMIT),
        cost_estimate=pl.CostEstimate(flops=flops, bytes_accessed=0, transcendentals=0),
        name="gate",
    )(*values, *after)


def whole_body(count, start, near, down, up, range_tiles, weights, offsets, az_taps, *rest):
    out, az_out, samples, turned = rest
    samples[...] = start[...]
    add_ends(near, down, up, samples)
    for block in range(count + 1):
        turned[block * BLK : (block + 1) * BLK, :] = compress(samples, range_tiles, block)
    for block in range(count):
        out[block * BLK : (block + 1) * BLK, :] = migrate(weights, offsets, turned, 0, block)
    toeplitz_tiles(az_taps, AZ_TILES, 0, az_out)


def whole_quarter(samples, near, down, up, range_tiles, weights, offsets, azimuth_ref):
    pulses = samples.shape[1]
    count = weights.shape[1] // BLK
    return call(
        functools.partial(whole_body, count),
        "whole_quarter",
        (bf16(count * BLK, 2 * pulses), bf16(AZ_TILES, WIDE, WIDE)),
        [VMEM()] * 8,
        (VMEM(),) * 2,
        [
            pltpu.VMEM(samples.shape, jnp.bfloat16),
            pltpu.VMEM(((count + 1) * BLK, 2 * pulses), jnp.bfloat16),
        ],
    )(samples, near, down, up, range_tiles, weights, offsets, azimuth_ref)


def azimuth_rows(bins, steps, parts, rows):
    me = lax.axis_index("pulse")
    for part, step in zip(parts, steps):
        rows[pl.ds(pl.multiple_of((me ^ step) * bins, bins), bins)] = part[...]


def azimuth_blocks(bins, count, rows, az_tiles, image, done=lambda block: None):
    reach = AZ_TILES // 2
    for block in range(count):
        low, high = max(0, reach - block), min(AZ_TILES, count + reach - block)
        window = jnp.concatenate(
            [
                rows[(block + tile - reach) * bins : (block + tile - reach + 1) * bins]
                for tile in range(low, high)
            ],
            axis=1,
        )
        total = jnp.dot(
            window,
            az_tiles[low:high].reshape((high - low) * WIDE, WIDE),
            preferred_element_type=jnp.float32,
        )
        for part in range(2):
            image[part, 0, :, block * BLK : (block + 1) * BLK] = total[
                :, part * BLK : (part + 1) * BLK
            ]
        done(block)


def column(image, out, sems, block):
    span = pl.ds(pl.multiple_of(block * BLK, BLK), BLK)
    return pltpu.make_async_copy(image.at[:, :, :, span], out.at[:, :, :, span], sems.at[block])


def azimuth_body(steps, az_tiles, *rest):
    *parts, out, rows, image, sems = rest
    bins = image.shape[2]
    count = image.shape[3] // BLK
    if steps:
        azimuth_rows(bins, steps, parts, rows)
    else:
        rows[...] = parts[0][...]
    azimuth_blocks(
        bins,
        count,
        rows,
        az_tiles,
        image,
        lambda block: column(image, out, sems, block).start(),
    )
    for block in range(count):
        column(image, out, sems, block).wait()


def azimuth(steps, count, az_tiles, parts):
    bins = sum(part.shape[0] for part in parts) // count
    shape = (2, 1, bins, count * BLK)
    return call(
        functools.partial(azimuth_body, steps),
        "azimuth",
        jax.ShapeDtypeStruct(shape, jnp.float32),
        [VMEM()] * (1 + len(parts)),
        HBM(),
        [
            pltpu.VMEM((count * bins, WIDE), jnp.bfloat16),
            pltpu.VMEM(shape, jnp.float32),
            pltpu.SemaphoreType.DMA((count,)),
        ],
    )(az_tiles, *parts)


def azimuth_most_body(steps, absent, az_tiles, *rest):
    *parts, image, rows = rest
    bins = image.shape[2]
    azimuth_rows(bins, [absent], [jnp.zeros((bins, WIDE), jnp.bfloat16)], rows)
    azimuth_rows(bins, steps, parts, rows)
    azimuth_blocks(bins, image.shape[3] // BLK, rows, az_tiles, image)


def azimuth_most(steps, absent, az_tiles, parts):
    bins = parts[0].shape[0]
    count = len(steps) + 1
    return call(
        functools.partial(azimuth_most_body, steps, absent),
        "azimuth_most",
        jax.ShapeDtypeStruct((2, 1, bins, count * BLK), jnp.float32),
        [VMEM()] * (1 + len(parts)),
        VMEM(),
        [pltpu.VMEM((count * bins, WIDE), jnp.bfloat16)],
    )(az_tiles, *parts)


def azimuth_last_body(step, az_tiles, most, part, out, image, sems):
    count = most.shape[3] // BLK
    low = (lax.axis_index("pulse") ^ step) - AZ_TILES // 2

    def move(source, place, block):
        span = pl.ds(pl.multiple_of(block * BLK, BLK), BLK)
        return pltpu.make_async_copy(
            source.at[:, :, :, pl.ds(pl.multiple_of(place * BLK, BLK), BLK)],
            out.at[:, :, :, span],
            sems.at[block],
        )

    for block in range(count):
        pl.when((block < low) | (block >= low + AZ_TILES))(move(most, block, block).start)
    for i in range(AZ_TILES):
        total = jnp.dot(
            part[...], az_tiles[AZ_TILES - 1 - i], preferred_element_type=jnp.float32
        )
        block = low + i
        held = pl.ds(pl.multiple_of(jnp.clip(block, 0, count - 1) * BLK, BLK), BLK)
        for side in range(2):
            image[side, 0, :, i * BLK : (i + 1) * BLK] = (
                most[side, 0, :, held] + total[:, side * BLK : (side + 1) * BLK]
            )
        inside = (block >= 0) & (block < count)
        pl.when(inside)(lambda i=i, block=block: move(image, i, block).start())
    for block in range(count):
        move(most, block, block).wait()


def azimuth_last(step, az_tiles, most, part):
    return call(
        functools.partial(azimuth_last_body, step),
        "azimuth_last",
        jax.ShapeDtypeStruct(most.shape, most.dtype),
        [VMEM()] * 3,
        HBM(),
        [
            pltpu.VMEM(most.shape[:3] + (AZ_TILES * BLK,), jnp.float32),
            pltpu.SemaphoreType.DMA((most.shape[3] // BLK,)),
        ],
    )(az_tiles, most, part)


def per_device(echoes, range_ref, band_weights, band_offsets, azimuth_ref):
    quarter_len = echoes.shape[2]
    peers = lax.axis_size("pulse")
    quarters = lax.axis_size("rng")
    bins = quarter_len // peers
    near, down, up = pack(echoes)
    cores = [(i, i + 1) for i in range(0, quarters - 1, 2)]
    chips = [(i, i + 1) for i in range(1, quarters - 1, 2)]
    near = lax.ppermute(near, "rng", cores + [(j, i) for i, j in cores])
    down = lax.ppermute(down, "rng", [(j, i) for i, j in chips])
    up = lax.ppermute(up, "rng", chips)
    weights, offsets = band_weights, band_offsets.reshape(-1, BLK)
    samples, range_tiles = prepare(echoes, range_ref)

    if bins != GROUP or peers != 8:
        mine, az_tiles = whole_quarter(
            samples, near, down, up, range_tiles, weights, offsets, azimuth_ref
        )
        swapped = lax.all_to_all(
            mine.reshape(peers, bins, WIDE), "pulse", split_axis=0, concat_axis=0, tiled=True
        )
        return azimuth(None, peers, az_tiles, [swapped.reshape(mine.shape)])

    def send(piece, k):
        return lax.ppermute(piece, "pulse", [(i, i ^ k) for i in range(peers)])

    samples, made = first_range(
        [4, 5], samples, near, down, up, range_tiles, weights, offsets
    )
    ready = dict(zip([4, 5], made))
    for some in [[6, 7], [2, 3], [1]]:
        made = next_range([some], made[0], samples, range_tiles, weights, offsets)
        ready.update(zip(some, made))
    parts = {}
    parts[4] = send(ready[4], 4)
    parts[5] = send(ready[5], 5)
    parts[6] = send(ready[6], 6)
    parts[7] = send(ready[7], 7)
    parts[3] = send(ready[3], 3)
    parts[1] = send(gate([ready[1]], (parts[5],))[0], 1)
    parts[2] = send(gate([ready[2]], (parts[4],))[0], 2)
    after = parts[5]
    parts[0], az_tiles = own_range(after, samples, range_tiles, weights, offsets, azimuth_ref)
    parts.update(zip([6, 7], gate((parts[6], parts[7],), (), 1000000000)))
    parts.update(zip([6, 7, 3], gate((parts[6], parts[7], parts[3],), (), 200000000)))
    last = parts.pop(2)
    most = azimuth_most(list(parts), 2, az_tiles, list(parts.values()))
    return azimuth_last(2, az_tiles, most, last)


def solution(mesh):
    return jax.shard_map(
        per_device,
        mesh=mesh,
        in_specs=(P(None, "pulse", "rng"), P(), P(None, "rng"), P("rng"), P()),
        out_specs=P(None, "rng", "pulse", None),
        check_vma=False,
    )
```

```python
import functools

import jax
import jax.numpy as jnp
from jax import lax
from jax.experimental import pallas as pl
from jax.experimental.pallas import tpu as pltpu
from jax.sharding import PartitionSpec as P

RT = 1024
AT = 512
BAND = 64
BLK = 128
HALF = BLK // 2
WIDE = 2 * BLK
RANGE_TILES = RT // BLK + 2
AZ_TILES = AT // BLK + 1
HEAD = RT // BLK + 1
GROUP = 2 * BLK
LIMIT = 24 * 1024 * 1024
PACK_FLOPS = 2 * 10**9
TILE_FLOPS = 2 * 10**9

VMEM = functools.partial(pl.BlockSpec, memory_space=pltpu.VMEM)
HBM = functools.partial(pl.BlockSpec, memory_space=pltpu.HBM)


def call(body, name, out_shape, in_specs, out_specs, scratch_shapes=(), flops=0):
    return pl.pallas_call(
        body,
        out_shape=out_shape,
        in_specs=in_specs,
        out_specs=out_specs,
        scratch_shapes=scratch_shapes,
        compiler_params=pltpu.CompilerParams(vmem_limit_bytes=LIMIT),
        cost_estimate=pl.CostEstimate(flops=flops, bytes_accessed=0, transcendentals=0),
        name=name,
    )


def bf16(*shape):
    return jax.ShapeDtypeStruct(shape, jnp.bfloat16)


def pack_body(echoes, after, near, down, up):
    odd = lax.axis_index("rng") % 2 == 1

    def block(part, place):
        return echoes[part, :, place * BLK : (place + 1) * BLK]

    def put_last(out):
        for part in range(2):
            out[0, :, part * BLK : (part + 1) * BLK] = block(part, echoes.shape[2] // BLK - 1)

    @pl.when(odd)
    def to_even():
        for part in range(2):
            for place in range(HEAD):
                near[place, :, part * BLK : (part + 1) * BLK] = block(part, place)
        put_last(up)

    @pl.when(jnp.logical_not(odd))
    def to_odd():
        for part in range(2):
            for place in range(HEAD - 1):
                down[2 * place + part] = block(part, place)
        lane = lax.broadcasted_iota(jnp.int32, near.shape[1:2] + (BLK,), 1)
        real, imag = (block(part, HEAD - 1).astype(jnp.float32) for part in range(2))
        joined = jnp.where(lane < HALF, real, pltpu.roll(imag, HALF, 1))
        down[2 * HEAD - 2] = joined.astype(jnp.bfloat16)
        put_last(near)


def pack(echoes, after):
    pulses = echoes.shape[1]
    return call(
        pack_body,
        "pack",
        (
            bf16(HEAD, pulses, WIDE),
            bf16(2 * HEAD - 1, pulses, BLK),
            bf16(1, pulses, WIDE),
        ),
        [VMEM()] * 2,
        (VMEM(),) * 3,
        flops=PACK_FLOPS,
    )(echoes, after)


def toeplitz_tiles(taps, tiles, shift, out):
    width = (tiles + 1) * BLK
    tap_total = taps.shape[1]
    skewed = []
    for part in range(2):
        row = jnp.concatenate(
            [
                jnp.zeros((1, BLK), jnp.float32),
                taps[part : part + 1, :].astype(jnp.float32),
                jnp.zeros((1, width - BLK - tap_total), jnp.float32),
            ],
            axis=1,
        )
        row = jnp.broadcast_to(row, (BLK, width))
        skewed.append(pltpu.roll(row, shift, 1, stride=1, stride_axis=0))
    for tile in range(tiles):
        span = slice((tile + 1) * BLK, (tile + 2) * BLK)
        real = skewed[0][:, span].T
        imag = skewed[1][:, span].T
        out[tile, :BLK, :BLK] = real.astype(jnp.bfloat16)
        out[tile, :BLK, BLK:] = (-imag).astype(jnp.bfloat16)
        out[tile, BLK:, :BLK] = imag.astype(jnp.bfloat16)
        out[tile, BLK:, BLK:] = real.astype(jnp.bfloat16)


def band(weights, offsets, block):
    span = pl.ds(pl.multiple_of(block * BLK, BLK), BLK)
    placed = jnp.concatenate(
        [weights[:, span].astype(jnp.float32), jnp.zeros((BLK - BAND, BLK), jnp.float32)], axis=0
    )
    shifts = offsets[pl.ds(block, 1), :]
    for bit in range((BAND // 2).bit_length()):
        chosen = jnp.broadcast_to((shifts >> bit) & 1, (BLK, BLK)) == 1
        placed = jnp.where(chosen, pltpu.roll(placed, 1 << bit, 0), placed)
    wide = jnp.concatenate([placed.T, jnp.zeros((BLK, BLK), jnp.float32)], axis=1)
    skewed = pltpu.roll(wide, BAND // 2, 1, stride=1, stride_axis=0)
    outside = (lax.axis_index("rng") == 0) & (block == 0)
    lane = lax.broadcasted_iota(jnp.int32, (BLK, WIDE), 1)
    return jnp.where(outside & (lane < HALF), 0.0, skewed).astype(jnp.bfloat16)


def range_tiles_body(range_ref, range_out):
    toeplitz_tiles(range_ref, RANGE_TILES, HALF, range_out)


def make_range_tiles(range_ref):
    return call(
        range_tiles_body,
        "range_tiles",
        bf16(RANGE_TILES, WIDE, WIDE),
        [VMEM()],
        VMEM(),
        flops=TILE_FLOPS,
    )(range_ref)


def lay_out_body(echoes, samples):
    for block in range(echoes.shape[2] // BLK):
        for part in range(2):
            samples[block + 1, :, part * BLK : (part + 1) * BLK] = echoes[
                part, :, block * BLK : (block + 1) * BLK
            ]


def lay_out(echoes):
    blocks = 1 + echoes.shape[2] // BLK + HEAD
    return call(
        lay_out_body, "lay_out", bf16(blocks, echoes.shape[1], WIDE), [VMEM()], VMEM()
    )(echoes)


def add_ends(near, down, up, out):
    start = out.shape[0] - HEAD
    odd = lax.axis_index("rng") % 2 == 1

    @pl.when(odd)
    def from_even():
        out[0] = near[0]
        for place in range(HEAD - 1):
            for part in range(2):
                out[start + place, :, part * BLK : (part + 1) * BLK] = down[2 * place + part]
        lane = lax.broadcasted_iota(jnp.int32, down.shape[1:], 1)
        joined = down[2 * HEAD - 2].astype(jnp.float32)
        for part, value in enumerate((joined, pltpu.roll(joined, HALF, 1))):
            out[start + HEAD - 1, :, part * BLK : (part + 1) * BLK] = jnp.where(
                lane < HALF, value, 0.0
            ).astype(jnp.bfloat16)

    @pl.when(jnp.logical_not(odd))
    def from_odd():
        out[0] = up[0]
        out[start:] = near[...]


def compress(samples, range_tiles, block):
    window = jnp.concatenate([samples[block + tile] for tile in range(RANGE_TILES)], axis=1)
    total = jnp.dot(
        window,
        range_tiles[...].reshape(RANGE_TILES * WIDE, WIDE),
        preferred_element_type=jnp.float32,
    ).astype(jnp.bfloat16)
    return jnp.concatenate([total[:, :BLK].T, total[:, BLK:].T], axis=1)


def migrate(weights, offsets, turned, first, place):
    reach = pl.multiple_of(place * BLK, BLK)
    return jnp.dot(
        band(weights, offsets, first + place),
        turned[pl.ds(reach, WIDE)],
        preferred_element_type=jnp.float32,
    ).astype(jnp.bfloat16)


def group_sends(steps, samples, range_tiles, weights, offsets, turned, outs):
    me = lax.axis_index("pulse")
    blocks = GROUP // BLK
    if len(steps) == 1:
        first, spots = blocks * (me ^ steps[0]), [0]
    else:
        first, spots = 2 * blocks * (me // 2 ^ steps[0] // 2), [me % 2 ^ k % 2 for k in steps]
    for block in range(blocks * len(steps) + 1):
        turned[block * BLK : (block + 1) * BLK, :] = compress(samples, range_tiles, first + block)
    for spot, out in zip(spots, outs):
        for block in range(blocks):
            out[block * BLK : (block + 1) * BLK, :] = migrate(
                weights, offsets, turned, first, spot * blocks + block
            )


def first_range_body(
    steps, start, near, down, up, range_tiles, weights, offsets, samples, *rest
):
    add_ends(near, down, up, samples)
    group_sends(steps, samples, range_tiles, weights, offsets, rest[-1], rest[:-1])


def first_range(steps, samples, near, down, up, range_tiles, weights, offsets):
    pulses = samples.shape[1]
    samples, *made = pl.pallas_call(
        functools.partial(first_range_body, steps),
        out_shape=(jax.ShapeDtypeStruct(samples.shape, samples.dtype),)
        + (bf16(GROUP, 2 * pulses),) * len(steps),
        in_specs=[VMEM()] * 7,
        out_specs=(VMEM(),) * (1 + len(steps)),
        scratch_shapes=[pltpu.VMEM((5 * BLK, 2 * pulses), jnp.bfloat16)],
        input_output_aliases={0: 0},
        compiler_params=pltpu.CompilerParams(vmem_limit_bytes=LIMIT),
        cost_estimate=pl.CostEstimate(flops=0, bytes_accessed=0, transcendentals=0),
        name="first_range",
    )(samples, near, down, up, range_tiles, weights, offsets)
    return samples, made


def next_range_body(steps, after, samples, range_tiles, weights, offsets, *rest):
    *outs, turned = rest
    done = row = 0
    for some in steps:
        size = len(some) * (GROUP // BLK) + 1
        group_sends(
            some,
            samples,
            range_tiles,
            weights,
            offsets,
            turned.at[pl.ds(row * BLK, size * BLK)],
            outs[done : done + len(some)],
        )
        done, row = done + len(some), row + size


def next_range(steps, after, samples, range_tiles, weights, offsets):
    pulses = samples.shape[1]
    count = sum(map(len, steps))
    size = count * (GROUP // BLK) + len(steps)
    return call(
        functools.partial(next_range_body, steps),
        "next_range",
        (bf16(GROUP, 2 * pulses),) * count,
        [VMEM()] * 5,
        (VMEM(),) * count,
        [pltpu.VMEM((size * BLK, 2 * pulses), jnp.bfloat16)],
    )(after, samples, range_tiles, weights, offsets)


def own_range_body(after, samples, range_tiles, weights, offsets, az_taps, out, az_out, turned):
    group_sends([0], samples, range_tiles, weights, offsets, turned, [out])
    toeplitz_tiles(az_taps, AZ_TILES, 0, az_out)


def own_range(after, samples, range_tiles, weights, offsets, azimuth_ref):
    pulses = samples.shape[1]
    return call(
        own_range_body,
        "own_range",
        (bf16(GROUP, 2 * pulses), bf16(AZ_TILES, WIDE, WIDE)),
        [VMEM()] * 6,
        (VMEM(),) * 2,
        [pltpu.VMEM((3 * BLK, 2 * pulses), jnp.bfloat16)],
    )(after, samples, range_tiles, weights, offsets, azimuth_ref)


def gate_body(*refs):
    pass


def gate(values, after=(), flops=0):
    whole = pl.BlockSpec(memory_space=pl.ANY)
    values = list(values)
    return pl.pallas_call(
        gate_body,
        out_shape=tuple(jax.ShapeDtypeStruct(value.shape, value.dtype) for value in values),
        in_specs=[whole] * (len(values) + len(after)),
        out_specs=(whole,) * len(values),
        input_output_aliases={i: i for i in range(len(values))},
        compiler_params=pltpu.CompilerParams(vmem_limit_bytes=LIMIT),
        cost_estimate=pl.CostEstimate(flops=flops, bytes_accessed=0, transcendentals=0),
        name="gate",
    )(*values, *after)


def whole_body(count, start, near, down, up, range_tiles, weights, offsets, az_taps, *rest):
    out, az_out, samples, turned = rest
    samples[...] = start[...]
    add_ends(near, down, up, samples)
    for block in range(count + 1):
        turned[block * BLK : (block + 1) * BLK, :] = compress(samples, range_tiles, block)
    for block in range(count):
        out[block * BLK : (block + 1) * BLK, :] = migrate(weights, offsets, turned, 0, block)
    toeplitz_tiles(az_taps, AZ_TILES, 0, az_out)


def whole_quarter(samples, near, down, up, range_tiles, weights, offsets, azimuth_ref):
    pulses = samples.shape[1]
    count = weights.shape[1] // BLK
    return call(
        functools.partial(whole_body, count),
        "whole_quarter",
        (bf16(count * BLK, 2 * pulses), bf16(AZ_TILES, WIDE, WIDE)),
        [VMEM()] * 8,
        (VMEM(),) * 2,
        [
            pltpu.VMEM(samples.shape, jnp.bfloat16),
            pltpu.VMEM(((count + 1) * BLK, 2 * pulses), jnp.bfloat16),
        ],
    )(samples, near, down, up, range_tiles, weights, offsets, azimuth_ref)


def azimuth_rows(bins, steps, parts, rows):
    me = lax.axis_index("pulse")
    for part, step in zip(parts, steps):
        rows[pl.ds(pl.multiple_of((me ^ step) * bins, bins), bins)] = part[...]


def azimuth_blocks(bins, count, rows, az_tiles, image, done=lambda block: None):
    reach = AZ_TILES // 2
    for block in range(count):
        low, high = max(0, reach - block), min(AZ_TILES, count + reach - block)
        window = jnp.concatenate(
            [
                rows[(block + tile - reach) * bins : (block + tile - reach + 1) * bins]
                for tile in range(low, high)
            ],
            axis=1,
        )
        total = jnp.dot(
            window,
            az_tiles[low:high].reshape((high - low) * WIDE, WIDE),
            preferred_element_type=jnp.float32,
        )
        for part in range(2):
            image[part, 0, :, block * BLK : (block + 1) * BLK] = total[
                :, part * BLK : (part + 1) * BLK
            ]
        done(block)


def column(image, out, sems, block):
    span = pl.ds(pl.multiple_of(block * BLK, BLK), BLK)
    return pltpu.make_async_copy(image.at[:, :, :, span], out.at[:, :, :, span], sems.at[block])


def azimuth_body(steps, az_tiles, *rest):
    *parts, out, rows, image, sems = rest
    bins = image.shape[2]
    count = image.shape[3] // BLK
    if steps:
        azimuth_rows(bins, steps, parts, rows)
    else:
        rows[...] = parts[0][...]
    azimuth_blocks(
        bins,
        count,
        rows,
        az_tiles,
        image,
        lambda block: column(image, out, sems, block).start(),
    )
    for block in range(count):
        column(image, out, sems, block).wait()


def azimuth(steps, count, az_tiles, parts):
    bins = sum(part.shape[0] for part in parts) // count
    shape = (2, 1, bins, count * BLK)
    return call(
        functools.partial(azimuth_body, steps),
        "azimuth",
        jax.ShapeDtypeStruct(shape, jnp.float32),
        [VMEM()] * (1 + len(parts)),
        HBM(),
        [
            pltpu.VMEM((count * bins, WIDE), jnp.bfloat16),
            pltpu.VMEM(shape, jnp.float32),
            pltpu.SemaphoreType.DMA((count,)),
        ],
    )(az_tiles, *parts)


def azimuth_most_body(steps, absent, az_tiles, *rest):
    *parts, image, rows = rest
    bins = image.shape[2]
    azimuth_rows(bins, [absent], [jnp.zeros((bins, WIDE), jnp.bfloat16)], rows)
    azimuth_rows(bins, steps, parts, rows)
    azimuth_blocks(bins, image.shape[3] // BLK, rows, az_tiles, image)


def azimuth_most(steps, absent, az_tiles, parts):
    bins = parts[0].shape[0]
    count = len(steps) + 1
    return call(
        functools.partial(azimuth_most_body, steps, absent),
        "azimuth_most",
        jax.ShapeDtypeStruct((2, 1, bins, count * BLK), jnp.float32),
        [VMEM()] * (1 + len(parts)),
        VMEM(),
        [pltpu.VMEM((count * bins, WIDE), jnp.bfloat16)],
    )(az_tiles, *parts)


def azimuth_last_body(step, az_tiles, most, part, out, image, sems):
    count = most.shape[3] // BLK
    low = (lax.axis_index("pulse") ^ step) - AZ_TILES // 2

    def move(source, place, block):
        span = pl.ds(pl.multiple_of(block * BLK, BLK), BLK)
        return pltpu.make_async_copy(
            source.at[:, :, :, pl.ds(pl.multiple_of(place * BLK, BLK), BLK)],
            out.at[:, :, :, span],
            sems.at[block],
        )

    for block in range(count):
        pl.when((block < low) | (block >= low + AZ_TILES))(move(most, block, block).start)
    for i in range(AZ_TILES):
        total = jnp.dot(
            part[...], az_tiles[AZ_TILES - 1 - i], preferred_element_type=jnp.float32
        )
        block = low + i
        held = pl.ds(pl.multiple_of(jnp.clip(block, 0, count - 1) * BLK, BLK), BLK)
        for side in range(2):
            image[side, 0, :, i * BLK : (i + 1) * BLK] = (
                most[side, 0, :, held] + total[:, side * BLK : (side + 1) * BLK]
            )
        inside = (block >= 0) & (block < count)
        pl.when(inside)(lambda i=i, block=block: move(image, i, block).start())
    for block in range(count):
        move(most, block, block).wait()


def azimuth_last(step, az_tiles, most, part):
    return call(
        functools.partial(azimuth_last_body, step),
        "azimuth_last",
        jax.ShapeDtypeStruct(most.shape, most.dtype),
        [VMEM()] * 3,
        HBM(),
        [
            pltpu.VMEM(most.shape[:3] + (AZ_TILES * BLK,), jnp.float32),
            pltpu.SemaphoreType.DMA((most.shape[3] // BLK,)),
        ],
    )(az_tiles, most, part)


def per_device(echoes, range_ref, band_weights, band_offsets, azimuth_ref):
    quarter_len = echoes.shape[2]
    peers = lax.axis_size("pulse")
    quarters = lax.axis_size("rng")
    bins = quarter_len // peers
    range_tiles = make_range_tiles(range_ref)
    near, down, up = pack(echoes, range_tiles)
    cores = [(i, i + 1) for i in range(0, quarters - 1, 2)]
    chips = [(i, i + 1) for i in range(1, quarters - 1, 2)]
    near = lax.ppermute(near, "rng", cores + [(j, i) for i, j in cores])
    down = lax.ppermute(down, "rng", [(j, i) for i, j in chips])
    up = lax.ppermute(up, "rng", chips)
    weights, offsets = band_weights, band_offsets.reshape(-1, BLK)
    samples = lay_out(echoes)

    if bins != GROUP or peers != 8:
        mine, az_tiles = whole_quarter(
            samples, near, down, up, range_tiles, weights, offsets, azimuth_ref
        )
        swapped = lax.all_to_all(
            mine.reshape(peers, bins, WIDE), "pulse", split_axis=0, concat_axis=0, tiled=True
        )
        return azimuth(None, peers, az_tiles, [swapped.reshape(mine.shape)])

    def send(piece, k):
        return lax.ppermute(piece, "pulse", [(i, i ^ k) for i in range(peers)])

    samples, made = first_range(
        [4, 5], samples, near, down, up, range_tiles, weights, offsets
    )
    ready = dict(zip([4, 5], made))
    for some in [[6, 7], [1], [2, 3]]:
        made = next_range([some], made[0], samples, range_tiles, weights, offsets)
        ready.update(zip(some, made))
    parts = {}
    parts[4] = send(ready[4], 4)
    parts[5] = send(ready[5], 5)
    parts[6] = send(ready[6], 6)
    parts[7] = send(ready[7], 7)
    parts[1] = send(ready[1], 1)
    parts[3] = send(gate([ready[3]], (parts[5],))[0], 3)
    parts[2] = send(gate([ready[2]], (parts[4],))[0], 2)
    after = parts[5]
    parts[0], az_tiles = own_range(after, samples, range_tiles, weights, offsets, azimuth_ref)
    parts.update(zip([6, 7], gate((parts[6], parts[7],), (), 1000000000)))
    parts.update(zip([6, 7, 1], gate((parts[6], parts[7], parts[1],), (), 200000000)))
    last = parts.pop(2)
    most = azimuth_most(list(parts), 2, az_tiles, list(parts.values()))
    return azimuth_last(2, az_tiles, most, last)


def solution(mesh):
    return jax.shard_map(
        per_device,
        mesh=mesh,
        in_specs=(P(None, "pulse", "rng"), P(), P(None, "rng"), P("rng"), P()),
        out_specs=P(None, "rng", "pulse", None),
        check_vma=False,
    )
```

```python
import functools

import jax
import jax.numpy as jnp
from jax import lax
from jax.experimental import pallas as pl
from jax.experimental.pallas import tpu as pltpu
from jax.sharding import PartitionSpec as P

RT = 1024
AT = 512
BAND = 64
BLK = 128
HALF = BLK // 2
WIDE = 2 * BLK
RANGE_TILES = RT // BLK + 2
AZ_TILES = AT // BLK + 1
HEAD = RT // BLK + 1
GROUP = 2 * BLK
LIMIT = 24 * 1024 * 1024
PACK_FLOPS = 2 * 10**9
TILE_FLOPS = 2 * 10**9

VMEM = functools.partial(pl.BlockSpec, memory_space=pltpu.VMEM)
HBM = functools.partial(pl.BlockSpec, memory_space=pltpu.HBM)


def call(body, name, out_shape, in_specs, out_specs, scratch_shapes=(), flops=0):
    return pl.pallas_call(
        body,
        out_shape=out_shape,
        in_specs=in_specs,
        out_specs=out_specs,
        scratch_shapes=scratch_shapes,
        compiler_params=pltpu.CompilerParams(vmem_limit_bytes=LIMIT),
        cost_estimate=pl.CostEstimate(flops=flops, bytes_accessed=0, transcendentals=0),
        name=name,
    )


def bf16(*shape):
    return jax.ShapeDtypeStruct(shape, jnp.bfloat16)


def pack_body(echoes, after, near, down, up):
    odd = lax.axis_index("rng") % 2 == 1

    def block(part, place):
        return echoes[part, :, place * BLK : (place + 1) * BLK]

    def put_last(out):
        for part in range(2):
            out[0, :, part * BLK : (part + 1) * BLK] = block(part, echoes.shape[2] // BLK - 1)

    @pl.when(odd)
    def to_even():
        for part in range(2):
            for place in range(HEAD):
                near[place, :, part * BLK : (part + 1) * BLK] = block(part, place)
        put_last(up)

    @pl.when(jnp.logical_not(odd))
    def to_odd():
        for part in range(2):
            for place in range(HEAD - 1):
                down[2 * place + part] = block(part, place)
        lane = lax.broadcasted_iota(jnp.int32, near.shape[1:2] + (BLK,), 1)
        real, imag = (block(part, HEAD - 1).astype(jnp.float32) for part in range(2))
        joined = jnp.where(lane < HALF, real, pltpu.roll(imag, HALF, 1))
        down[2 * HEAD - 2] = joined.astype(jnp.bfloat16)
        put_last(near)


def pack(echoes, after):
    pulses = echoes.shape[1]
    return call(
        pack_body,
        "pack",
        (
            bf16(HEAD, pulses, WIDE),
            bf16(2 * HEAD - 1, pulses, BLK),
            bf16(1, pulses, WIDE),
        ),
        [VMEM()] * 2,
        (VMEM(),) * 3,
        flops=PACK_FLOPS,
    )(echoes, after)


def toeplitz_tiles(taps, tiles, shift, out):
    width = (tiles + 1) * BLK
    tap_total = taps.shape[1]
    skewed = []
    for part in range(2):
        row = jnp.concatenate(
            [
                jnp.zeros((1, BLK), jnp.float32),
                taps[part : part + 1, :].astype(jnp.float32),
                jnp.zeros((1, width - BLK - tap_total), jnp.float32),
            ],
            axis=1,
        )
        row = jnp.broadcast_to(row, (BLK, width))
        skewed.append(pltpu.roll(row, shift, 1, stride=1, stride_axis=0))
    for tile in range(tiles):
        span = slice((tile + 1) * BLK, (tile + 2) * BLK)
        real = skewed[0][:, span].T
        imag = skewed[1][:, span].T
        out[tile, :BLK, :BLK] = real.astype(jnp.bfloat16)
        out[tile, :BLK, BLK:] = (-imag).astype(jnp.bfloat16)
        out[tile, BLK:, :BLK] = imag.astype(jnp.bfloat16)
        out[tile, BLK:, BLK:] = real.astype(jnp.bfloat16)


def band(weights, offsets, block):
    span = pl.ds(pl.multiple_of(block * BLK, BLK), BLK)
    placed = jnp.concatenate(
        [weights[:, span].astype(jnp.float32), jnp.zeros((BLK - BAND, BLK), jnp.float32)], axis=0
    )
    shifts = offsets[pl.ds(block, 1), :]
    for bit in range((BAND // 2).bit_length()):
        chosen = jnp.broadcast_to((shifts >> bit) & 1, (BLK, BLK)) == 1
        placed = jnp.where(chosen, pltpu.roll(placed, 1 << bit, 0), placed)
    wide = jnp.concatenate([placed.T, jnp.zeros((BLK, BLK), jnp.float32)], axis=1)
    skewed = pltpu.roll(wide, BAND // 2, 1, stride=1, stride_axis=0)
    outside = (lax.axis_index("rng") == 0) & (block == 0)
    lane = lax.broadcasted_iota(jnp.int32, (BLK, WIDE), 1)
    return jnp.where(outside & (lane < HALF), 0.0, skewed).astype(jnp.bfloat16)


def range_tiles_body(range_ref, range_out):
    toeplitz_tiles(range_ref, RANGE_TILES, HALF, range_out)


def make_range_tiles(range_ref):
    return call(
        range_tiles_body,
        "range_tiles",
        bf16(RANGE_TILES, WIDE, WIDE),
        [VMEM()],
        VMEM(),
        flops=TILE_FLOPS,
    )(range_ref)


def lay_out_body(echoes, samples):
    for block in range(echoes.shape[2] // BLK):
        for part in range(2):
            samples[block + 1, :, part * BLK : (part + 1) * BLK] = echoes[
                part, :, block * BLK : (block + 1) * BLK
            ]


def lay_out(echoes):
    blocks = 1 + echoes.shape[2] // BLK + HEAD
    return call(
        lay_out_body, "lay_out", bf16(blocks, echoes.shape[1], WIDE), [VMEM()], VMEM()
    )(echoes)


def add_ends(near, down, up, out):
    start = out.shape[0] - HEAD
    odd = lax.axis_index("rng") % 2 == 1

    @pl.when(odd)
    def from_even():
        out[0] = near[0]
        for place in range(HEAD - 1):
            for part in range(2):
                out[start + place, :, part * BLK : (part + 1) * BLK] = down[2 * place + part]
        lane = lax.broadcasted_iota(jnp.int32, down.shape[1:], 1)
        joined = down[2 * HEAD - 2].astype(jnp.float32)
        for part, value in enumerate((joined, pltpu.roll(joined, HALF, 1))):
            out[start + HEAD - 1, :, part * BLK : (part + 1) * BLK] = jnp.where(
                lane < HALF, value, 0.0
            ).astype(jnp.bfloat16)

    @pl.when(jnp.logical_not(odd))
    def from_odd():
        out[0] = up[0]
        out[start:] = near[...]


def compress(samples, range_tiles, block):
    window = jnp.concatenate([samples[block + tile] for tile in range(RANGE_TILES)], axis=1)
    total = jnp.dot(
        window,
        range_tiles[...].reshape(RANGE_TILES * WIDE, WIDE),
        preferred_element_type=jnp.float32,
    ).astype(jnp.bfloat16)
    return jnp.concatenate([total[:, :BLK].T, total[:, BLK:].T], axis=1)


def migrate(weights, offsets, turned, first, place):
    reach = pl.multiple_of(place * BLK, BLK)
    return jnp.dot(
        band(weights, offsets, first + place),
        turned[pl.ds(reach, WIDE)],
        preferred_element_type=jnp.float32,
    ).astype(jnp.bfloat16)


def group_sends(steps, samples, range_tiles, weights, offsets, turned, outs):
    me = lax.axis_index("pulse")
    blocks = GROUP // BLK
    if len(steps) == 1:
        first, spots = blocks * (me ^ steps[0]), [0]
    else:
        first, spots = 2 * blocks * (me // 2 ^ steps[0] // 2), [me % 2 ^ k % 2 for k in steps]
    for block in range(blocks * len(steps) + 1):
        turned[block * BLK : (block + 1) * BLK, :] = compress(samples, range_tiles, first + block)
    for spot, out in zip(spots, outs):
        for block in range(blocks):
            out[block * BLK : (block + 1) * BLK, :] = migrate(
                weights, offsets, turned, first, spot * blocks + block
            )


def first_range_body(
    steps, start, near, down, up, range_tiles, weights, offsets, samples, *rest
):
    add_ends(near, down, up, samples)
    group_sends(steps, samples, range_tiles, weights, offsets, rest[-1], rest[:-1])


def first_range(steps, samples, near, down, up, range_tiles, weights, offsets):
    pulses = samples.shape[1]
    samples, *made = pl.pallas_call(
        functools.partial(first_range_body, steps),
        out_shape=(jax.ShapeDtypeStruct(samples.shape, samples.dtype),)
        + (bf16(GROUP, 2 * pulses),) * len(steps),
        in_specs=[VMEM()] * 7,
        out_specs=(VMEM(),) * (1 + len(steps)),
        scratch_shapes=[pltpu.VMEM((5 * BLK, 2 * pulses), jnp.bfloat16)],
        input_output_aliases={0: 0},
        compiler_params=pltpu.CompilerParams(vmem_limit_bytes=LIMIT),
        cost_estimate=pl.CostEstimate(flops=0, bytes_accessed=0, transcendentals=0),
        name="first_range",
    )(samples, near, down, up, range_tiles, weights, offsets)
    return samples, made


def next_range_body(steps, after, samples, range_tiles, weights, offsets, *rest):
    *outs, turned = rest
    done = row = 0
    for some in steps:
        size = len(some) * (GROUP // BLK) + 1
        group_sends(
            some,
            samples,
            range_tiles,
            weights,
            offsets,
            turned.at[pl.ds(row * BLK, size * BLK)],
            outs[done : done + len(some)],
        )
        done, row = done + len(some), row + size


def next_range(steps, after, samples, range_tiles, weights, offsets):
    pulses = samples.shape[1]
    count = sum(map(len, steps))
    size = count * (GROUP // BLK) + len(steps)
    return call(
        functools.partial(next_range_body, steps),
        "next_range",
        (bf16(GROUP, 2 * pulses),) * count,
        [VMEM()] * 5,
        (VMEM(),) * count,
        [pltpu.VMEM((size * BLK, 2 * pulses), jnp.bfloat16)],
    )(after, samples, range_tiles, weights, offsets)


def own_range_body(after, samples, range_tiles, weights, offsets, az_taps, out, az_out, turned):
    group_sends([0], samples, range_tiles, weights, offsets, turned, [out])
    toeplitz_tiles(az_taps, AZ_TILES, 0, az_out)


def own_range(after, samples, range_tiles, weights, offsets, azimuth_ref):
    pulses = samples.shape[1]
    return call(
        own_range_body,
        "own_range",
        (bf16(GROUP, 2 * pulses), bf16(AZ_TILES, WIDE, WIDE)),
        [VMEM()] * 6,
        (VMEM(),) * 2,
        [pltpu.VMEM((3 * BLK, 2 * pulses), jnp.bfloat16)],
    )(after, samples, range_tiles, weights, offsets, azimuth_ref)


def gate_body(*refs):
    pass


def gate(values, after=(), flops=0):
    whole = pl.BlockSpec(memory_space=pl.ANY)
    values = list(values)
    return pl.pallas_call(
        gate_body,
        out_shape=tuple(jax.ShapeDtypeStruct(value.shape, value.dtype) for value in values),
        in_specs=[whole] * (len(values) + len(after)),
        out_specs=(whole,) * len(values),
        input_output_aliases={i: i for i in range(len(values))},
        compiler_params=pltpu.CompilerParams(vmem_limit_bytes=LIMIT),
        cost_estimate=pl.CostEstimate(flops=flops, bytes_accessed=0, transcendentals=0),
        name="gate",
    )(*values, *after)


def whole_body(count, start, near, down, up, range_tiles, weights, offsets, az_taps, *rest):
    out, az_out, samples, turned = rest
    samples[...] = start[...]
    add_ends(near, down, up, samples)
    for block in range(count + 1):
        turned[block * BLK : (block + 1) * BLK, :] = compress(samples, range_tiles, block)
    for block in range(count):
        out[block * BLK : (block + 1) * BLK, :] = migrate(weights, offsets, turned, 0, block)
    toeplitz_tiles(az_taps, AZ_TILES, 0, az_out)


def whole_quarter(samples, near, down, up, range_tiles, weights, offsets, azimuth_ref):
    pulses = samples.shape[1]
    count = weights.shape[1] // BLK
    return call(
        functools.partial(whole_body, count),
        "whole_quarter",
        (bf16(count * BLK, 2 * pulses), bf16(AZ_TILES, WIDE, WIDE)),
        [VMEM()] * 8,
        (VMEM(),) * 2,
        [
            pltpu.VMEM(samples.shape, jnp.bfloat16),
            pltpu.VMEM(((count + 1) * BLK, 2 * pulses), jnp.bfloat16),
        ],
    )(samples, near, down, up, range_tiles, weights, offsets, azimuth_ref)


def azimuth_rows(bins, steps, parts, rows):
    me = lax.axis_index("pulse")
    for part, step in zip(parts, steps):
        rows[pl.ds(pl.multiple_of((me ^ step) * bins, bins), bins)] = part[...]


def azimuth_blocks(bins, count, rows, az_tiles, image, done=lambda block: None):
    reach = AZ_TILES // 2
    for block in range(count):
        low, high = max(0, reach - block), min(AZ_TILES, count + reach - block)
        window = jnp.concatenate(
            [
                rows[(block + tile - reach) * bins : (block + tile - reach + 1) * bins]
                for tile in range(low, high)
            ],
            axis=1,
        )
        total = jnp.dot(
            window,
            az_tiles[low:high].reshape((high - low) * WIDE, WIDE),
            preferred_element_type=jnp.float32,
        )
        for part in range(2):
            image[part, 0, :, block * BLK : (block + 1) * BLK] = total[
                :, part * BLK : (part + 1) * BLK
            ]
        done(block)


def column(image, out, sems, block):
    span = pl.ds(pl.multiple_of(block * BLK, BLK), BLK)
    return pltpu.make_async_copy(image.at[:, :, :, span], out.at[:, :, :, span], sems.at[block])


def azimuth_body(steps, az_tiles, *rest):
    *parts, out, rows, image, sems = rest
    bins = image.shape[2]
    count = image.shape[3] // BLK
    if steps:
        azimuth_rows(bins, steps, parts, rows)
    else:
        rows[...] = parts[0][...]
    azimuth_blocks(
        bins,
        count,
        rows,
        az_tiles,
        image,
        lambda block: column(image, out, sems, block).start(),
    )
    for block in range(count):
        column(image, out, sems, block).wait()


def azimuth(steps, count, az_tiles, parts):
    bins = sum(part.shape[0] for part in parts) // count
    shape = (2, 1, bins, count * BLK)
    return call(
        functools.partial(azimuth_body, steps),
        "azimuth",
        jax.ShapeDtypeStruct(shape, jnp.float32),
        [VMEM()] * (1 + len(parts)),
        HBM(),
        [
            pltpu.VMEM((count * bins, WIDE), jnp.bfloat16),
            pltpu.VMEM(shape, jnp.float32),
            pltpu.SemaphoreType.DMA((count,)),
        ],
    )(az_tiles, *parts)


def azimuth_most_body(steps, absent, az_tiles, *rest):
    *parts, image, rows = rest
    bins = image.shape[2]
    azimuth_rows(bins, [absent], [jnp.zeros((bins, WIDE), jnp.bfloat16)], rows)
    azimuth_rows(bins, steps, parts, rows)
    azimuth_blocks(bins, image.shape[3] // BLK, rows, az_tiles, image)


def azimuth_most(steps, absent, az_tiles, parts):
    bins = parts[0].shape[0]
    count = len(steps) + 1
    return call(
        functools.partial(azimuth_most_body, steps, absent),
        "azimuth_most",
        jax.ShapeDtypeStruct((2, 1, bins, count * BLK), jnp.float32),
        [VMEM()] * (1 + len(parts)),
        VMEM(),
        [pltpu.VMEM((count * bins, WIDE), jnp.bfloat16)],
    )(az_tiles, *parts)


def azimuth_last_body(step, az_tiles, most, part, out, image, sems):
    count = most.shape[3] // BLK
    low = (lax.axis_index("pulse") ^ step) - AZ_TILES // 2

    def move(source, place, block):
        span = pl.ds(pl.multiple_of(block * BLK, BLK), BLK)
        return pltpu.make_async_copy(
            source.at[:, :, :, pl.ds(pl.multiple_of(place * BLK, BLK), BLK)],
            out.at[:, :, :, span],
            sems.at[block],
        )

    for block in range(count):
        pl.when((block < low) | (block >= low + AZ_TILES))(move(most, block, block).start)
    for i in range(AZ_TILES):
        total = jnp.dot(
            part[...], az_tiles[AZ_TILES - 1 - i], preferred_element_type=jnp.float32
        )
        block = low + i
        held = pl.ds(pl.multiple_of(jnp.clip(block, 0, count - 1) * BLK, BLK), BLK)
        for side in range(2):
            image[side, 0, :, i * BLK : (i + 1) * BLK] = (
                most[side, 0, :, held] + total[:, side * BLK : (side + 1) * BLK]
            )
        inside = (block >= 0) & (block < count)
        pl.when(inside)(lambda i=i, block=block: move(image, i, block).start())
    for block in range(count):
        move(most, block, block).wait()


def azimuth_last(step, az_tiles, most, part):
    return call(
        functools.partial(azimuth_last_body, step),
        "azimuth_last",
        jax.ShapeDtypeStruct(most.shape, most.dtype),
        [VMEM()] * 3,
        HBM(),
        [
            pltpu.VMEM(most.shape[:3] + (AZ_TILES * BLK,), jnp.float32),
            pltpu.SemaphoreType.DMA((most.shape[3] // BLK,)),
        ],
    )(az_tiles, most, part)


def per_device(echoes, range_ref, band_weights, band_offsets, azimuth_ref):
    quarter_len = echoes.shape[2]
    peers = lax.axis_size("pulse")
    quarters = lax.axis_size("rng")
    bins = quarter_len // peers
    range_tiles = make_range_tiles(range_ref)
    near, down, up = pack(echoes, range_tiles)
    cores = [(i, i + 1) for i in range(0, quarters - 1, 2)]
    chips = [(i, i + 1) for i in range(1, quarters - 1, 2)]
    near = lax.ppermute(near, "rng", cores + [(j, i) for i, j in cores])
    down = lax.ppermute(down, "rng", [(j, i) for i, j in chips])
    up = lax.ppermute(up, "rng", chips)
    weights, offsets = band_weights, band_offsets.reshape(-1, BLK)
    samples = lay_out(echoes)

    if bins != GROUP or peers != 8:
        mine, az_tiles = whole_quarter(
            samples, near, down, up, range_tiles, weights, offsets, azimuth_ref
        )
        swapped = lax.all_to_all(
            mine.reshape(peers, bins, WIDE), "pulse", split_axis=0, concat_axis=0, tiled=True
        )
        return azimuth(None, peers, az_tiles, [swapped.reshape(mine.shape)])

    def send(piece, k):
        return lax.ppermute(piece, "pulse", [(i, i ^ k) for i in range(peers)])

    samples, made = first_range(
        [4, 5], samples, near, down, up, range_tiles, weights, offsets
    )
    ready = dict(zip([4, 5], made))
    for some in [[6, 7], [1], [2, 3]]:
        made = next_range([some], made[0], samples, range_tiles, weights, offsets)
        ready.update(zip(some, made))
    parts = {}
    parts[4] = send(ready[4], 4)
    parts[5] = send(ready[5], 5)
    parts[6] = send(ready[6], 6)
    parts[7] = send(ready[7], 7)
    parts[1] = send(ready[1], 1)
    parts[3] = send(gate([ready[3]], (parts[5],))[0], 3)
    parts[2] = send(gate([ready[2]], (parts[4],))[0], 2)
    after = parts[6]
    parts[0], az_tiles = own_range(after, samples, range_tiles, weights, offsets, azimuth_ref)
    parts.update(zip([6, 7], gate((parts[6], parts[7],), (), 1000000000)))
    parts.update(zip([6, 7, 1], gate((parts[6], parts[7], parts[1],), (), 200000000)))
    last = parts.pop(2)
    most = azimuth_most(list(parts), 2, az_tiles, list(parts.values()))
    return azimuth_last(2, az_tiles, most, last)


def solution(mesh):
    return jax.shard_map(
        per_device,
        mesh=mesh,
        in_specs=(P(None, "pulse", "rng"), P(), P(None, "rng"), P("rng"), P()),
        out_specs=P(None, "rng", "pulse", None),
        check_vma=False,
    )
```

```python
import functools

import jax
import jax.numpy as jnp
from jax import lax
from jax.experimental import pallas as pl
from jax.experimental.pallas import tpu as pltpu
from jax.sharding import PartitionSpec as P

RT = 1024
AT = 512
BAND = 64
BLK = 128
HALF = BLK // 2
WIDE = 2 * BLK
RANGE_TILES = RT // BLK + 2
AZ_TILES = AT // BLK + 1
HEAD = RT // BLK + 1
GROUP = 2 * BLK
LIMIT = 24 * 1024 * 1024
PACK_FLOPS = 2 * 10**9
TILE_FLOPS = 2 * 10**9

VMEM = functools.partial(pl.BlockSpec, memory_space=pltpu.VMEM)
HBM = functools.partial(pl.BlockSpec, memory_space=pltpu.HBM)


def call(body, name, out_shape, in_specs, out_specs, scratch_shapes=(), flops=0):
    return pl.pallas_call(
        body,
        out_shape=out_shape,
        in_specs=in_specs,
        out_specs=out_specs,
        scratch_shapes=scratch_shapes,
        compiler_params=pltpu.CompilerParams(vmem_limit_bytes=LIMIT),
        cost_estimate=pl.CostEstimate(flops=flops, bytes_accessed=0, transcendentals=0),
        name=name,
    )


def bf16(*shape):
    return jax.ShapeDtypeStruct(shape, jnp.bfloat16)


def pack_body(echoes, after, near, down, up):
    odd = lax.axis_index("rng") % 2 == 1

    def block(part, place):
        return echoes[part, :, place * BLK : (place + 1) * BLK]

    def put_last(out):
        for part in range(2):
            out[0, :, part * BLK : (part + 1) * BLK] = block(part, echoes.shape[2] // BLK - 1)

    @pl.when(odd)
    def to_even():
        for part in range(2):
            for place in range(HEAD):
                near[place, :, part * BLK : (part + 1) * BLK] = block(part, place)
        put_last(up)

    @pl.when(jnp.logical_not(odd))
    def to_odd():
        for part in range(2):
            for place in range(HEAD - 1):
                down[2 * place + part] = block(part, place)
        lane = lax.broadcasted_iota(jnp.int32, near.shape[1:2] + (BLK,), 1)
        real, imag = (block(part, HEAD - 1).astype(jnp.float32) for part in range(2))
        joined = jnp.where(lane < HALF, real, pltpu.roll(imag, HALF, 1))
        down[2 * HEAD - 2] = joined.astype(jnp.bfloat16)
        put_last(near)


def pack(echoes, after):
    pulses = echoes.shape[1]
    return call(
        pack_body,
        "pack",
        (
            bf16(HEAD, pulses, WIDE),
            bf16(2 * HEAD - 1, pulses, BLK),
            bf16(1, pulses, WIDE),
        ),
        [VMEM()] * 2,
        (VMEM(),) * 3,
        flops=PACK_FLOPS,
    )(echoes, after)


def toeplitz_tiles(taps, tiles, shift, out):
    width = (tiles + 1) * BLK
    tap_total = taps.shape[1]
    skewed = []
    for part in range(2):
        row = jnp.concatenate(
            [
                jnp.zeros((1, BLK), jnp.float32),
                taps[part : part + 1, :].astype(jnp.float32),
                jnp.zeros((1, width - BLK - tap_total), jnp.float32),
            ],
            axis=1,
        )
        row = jnp.broadcast_to(row, (BLK, width))
        skewed.append(pltpu.roll(row, shift, 1, stride=1, stride_axis=0))
    for tile in range(tiles):
        span = slice((tile + 1) * BLK, (tile + 2) * BLK)
        real = skewed[0][:, span].T
        imag = skewed[1][:, span].T
        out[tile, :BLK, :BLK] = real.astype(jnp.bfloat16)
        out[tile, :BLK, BLK:] = (-imag).astype(jnp.bfloat16)
        out[tile, BLK:, :BLK] = imag.astype(jnp.bfloat16)
        out[tile, BLK:, BLK:] = real.astype(jnp.bfloat16)


def band(weights, offsets, block):
    span = pl.ds(pl.multiple_of(block * BLK, BLK), BLK)
    placed = jnp.concatenate(
        [weights[:, span].astype(jnp.float32), jnp.zeros((BLK - BAND, BLK), jnp.float32)], axis=0
    )
    shifts = offsets[pl.ds(block, 1), :]
    for bit in range((BAND // 2).bit_length()):
        chosen = jnp.broadcast_to((shifts >> bit) & 1, (BLK, BLK)) == 1
        placed = jnp.where(chosen, pltpu.roll(placed, 1 << bit, 0), placed)
    wide = jnp.concatenate([placed.T, jnp.zeros((BLK, BLK), jnp.float32)], axis=1)
    skewed = pltpu.roll(wide, BAND // 2, 1, stride=1, stride_axis=0)
    outside = (lax.axis_index("rng") == 0) & (block == 0)
    lane = lax.broadcasted_iota(jnp.int32, (BLK, WIDE), 1)
    return jnp.where(outside & (lane < HALF), 0.0, skewed).astype(jnp.bfloat16)


def range_tiles_body(range_ref, range_out):
    toeplitz_tiles(range_ref, RANGE_TILES, HALF, range_out)


def make_range_tiles(range_ref):
    return call(
        range_tiles_body,
        "range_tiles",
        bf16(RANGE_TILES, WIDE, WIDE),
        [VMEM()],
        VMEM(),
        flops=TILE_FLOPS,
    )(range_ref)


def lay_out_body(echoes, samples):
    for block in range(echoes.shape[2] // BLK):
        for part in range(2):
            samples[block + 1, :, part * BLK : (part + 1) * BLK] = echoes[
                part, :, block * BLK : (block + 1) * BLK
            ]


def lay_out(echoes):
    blocks = 1 + echoes.shape[2] // BLK + HEAD
    return call(
        lay_out_body, "lay_out", bf16(blocks, echoes.shape[1], WIDE), [VMEM()], VMEM()
    )(echoes)


def add_ends(near, down, up, out):
    start = out.shape[0] - HEAD
    odd = lax.axis_index("rng") % 2 == 1

    @pl.when(odd)
    def from_even():
        out[0] = near[0]
        for place in range(HEAD - 1):
            for part in range(2):
                out[start + place, :, part * BLK : (part + 1) * BLK] = down[2 * place + part]
        lane = lax.broadcasted_iota(jnp.int32, down.shape[1:], 1)
        joined = down[2 * HEAD - 2].astype(jnp.float32)
        for part, value in enumerate((joined, pltpu.roll(joined, HALF, 1))):
            out[start + HEAD - 1, :, part * BLK : (part + 1) * BLK] = jnp.where(
                lane < HALF, value, 0.0
            ).astype(jnp.bfloat16)

    @pl.when(jnp.logical_not(odd))
    def from_odd():
        out[0] = up[0]
        out[start:] = near[...]


def compress(samples, range_tiles, block):
    window = jnp.concatenate([samples[block + tile] for tile in range(RANGE_TILES)], axis=1)
    total = jnp.dot(
        window,
        range_tiles[...].reshape(RANGE_TILES * WIDE, WIDE),
        preferred_element_type=jnp.float32,
    ).astype(jnp.bfloat16)
    return jnp.concatenate([total[:, :BLK].T, total[:, BLK:].T], axis=1)


def migrate(weights, offsets, turned, first, place):
    reach = pl.multiple_of(place * BLK, BLK)
    return jnp.dot(
        band(weights, offsets, first + place),
        turned[pl.ds(reach, WIDE)],
        preferred_element_type=jnp.float32,
    ).astype(jnp.bfloat16)


def group_sends(steps, samples, range_tiles, weights, offsets, turned, outs):
    me = lax.axis_index("pulse")
    blocks = GROUP // BLK
    if len(steps) == 1:
        first, spots = blocks * (me ^ steps[0]), [0]
    else:
        first, spots = 2 * blocks * (me // 2 ^ steps[0] // 2), [me % 2 ^ k % 2 for k in steps]
    for block in range(blocks * len(steps) + 1):
        turned[block * BLK : (block + 1) * BLK, :] = compress(samples, range_tiles, first + block)
    for spot, out in zip(spots, outs):
        for block in range(blocks):
            out[block * BLK : (block + 1) * BLK, :] = migrate(
                weights, offsets, turned, first, spot * blocks + block
            )


def first_range_body(
    steps, start, near, down, up, range_tiles, weights, offsets, samples, *rest
):
    add_ends(near, down, up, samples)
    group_sends(steps, samples, range_tiles, weights, offsets, rest[-1], rest[:-1])


def first_range(steps, samples, near, down, up, range_tiles, weights, offsets):
    pulses = samples.shape[1]
    samples, *made = pl.pallas_call(
        functools.partial(first_range_body, steps),
        out_shape=(jax.ShapeDtypeStruct(samples.shape, samples.dtype),)
        + (bf16(GROUP, 2 * pulses),) * len(steps),
        in_specs=[VMEM()] * 7,
        out_specs=(VMEM(),) * (1 + len(steps)),
        scratch_shapes=[pltpu.VMEM((5 * BLK, 2 * pulses), jnp.bfloat16)],
        input_output_aliases={0: 0},
        compiler_params=pltpu.CompilerParams(vmem_limit_bytes=LIMIT),
        cost_estimate=pl.CostEstimate(flops=0, bytes_accessed=0, transcendentals=0),
        name="first_range",
    )(samples, near, down, up, range_tiles, weights, offsets)
    return samples, made


def next_range_body(steps, after, samples, range_tiles, weights, offsets, *rest):
    *outs, turned = rest
    done = row = 0
    for some in steps:
        size = len(some) * (GROUP // BLK) + 1
        group_sends(
            some,
            samples,
            range_tiles,
            weights,
            offsets,
            turned.at[pl.ds(row * BLK, size * BLK)],
            outs[done : done + len(some)],
        )
        done, row = done + len(some), row + size


def next_range(steps, after, samples, range_tiles, weights, offsets):
    pulses = samples.shape[1]
    count = sum(map(len, steps))
    size = count * (GROUP // BLK) + len(steps)
    return call(
        functools.partial(next_range_body, steps),
        "next_range",
        (bf16(GROUP, 2 * pulses),) * count,
        [VMEM()] * 5,
        (VMEM(),) * count,
        [pltpu.VMEM((size * BLK, 2 * pulses), jnp.bfloat16)],
    )(after, samples, range_tiles, weights, offsets)


def own_range_body(after, samples, range_tiles, weights, offsets, az_taps, out, az_out, turned):
    group_sends([0], samples, range_tiles, weights, offsets, turned, [out])
    toeplitz_tiles(az_taps, AZ_TILES, 0, az_out)


def own_range(after, samples, range_tiles, weights, offsets, azimuth_ref):
    pulses = samples.shape[1]
    return call(
        own_range_body,
        "own_range",
        (bf16(GROUP, 2 * pulses), bf16(AZ_TILES, WIDE, WIDE)),
        [VMEM()] * 6,
        (VMEM(),) * 2,
        [pltpu.VMEM((3 * BLK, 2 * pulses), jnp.bfloat16)],
    )(after, samples, range_tiles, weights, offsets, azimuth_ref)


def gate_body(*refs):
    pass


def gate(values, after=(), flops=0):
    whole = pl.BlockSpec(memory_space=pl.ANY)
    values = list(values)
    return pl.pallas_call(
        gate_body,
        out_shape=tuple(jax.ShapeDtypeStruct(value.shape, value.dtype) for value in values),
        in_specs=[whole] * (len(values) + len(after)),
        out_specs=(whole,) * len(values),
        input_output_aliases={i: i for i in range(len(values))},
        compiler_params=pltpu.CompilerParams(vmem_limit_bytes=LIMIT),
        cost_estimate=pl.CostEstimate(flops=flops, bytes_accessed=0, transcendentals=0),
        name="gate",
    )(*values, *after)


def whole_body(count, start, near, down, up, range_tiles, weights, offsets, az_taps, *rest):
    out, az_out, samples, turned = rest
    samples[...] = start[...]
    add_ends(near, down, up, samples)
    for block in range(count + 1):
        turned[block * BLK : (block + 1) * BLK, :] = compress(samples, range_tiles, block)
    for block in range(count):
        out[block * BLK : (block + 1) * BLK, :] = migrate(weights, offsets, turned, 0, block)
    toeplitz_tiles(az_taps, AZ_TILES, 0, az_out)


def whole_quarter(samples, near, down, up, range_tiles, weights, offsets, azimuth_ref):
    pulses = samples.shape[1]
    count = weights.shape[1] // BLK
    return call(
        functools.partial(whole_body, count),
        "whole_quarter",
        (bf16(count * BLK, 2 * pulses), bf16(AZ_TILES, WIDE, WIDE)),
        [VMEM()] * 8,
        (VMEM(),) * 2,
        [
            pltpu.VMEM(samples.shape, jnp.bfloat16),
            pltpu.VMEM(((count + 1) * BLK, 2 * pulses), jnp.bfloat16),
        ],
    )(samples, near, down, up, range_tiles, weights, offsets, azimuth_ref)


def azimuth_rows(bins, steps, parts, rows):
    me = lax.axis_index("pulse")
    for part, step in zip(parts, steps):
        rows[pl.ds(pl.multiple_of((me ^ step) * bins, bins), bins)] = part[...]


def azimuth_blocks(bins, count, rows, az_tiles, image, done=lambda block: None):
    reach = AZ_TILES // 2
    for block in range(count):
        low, high = max(0, reach - block), min(AZ_TILES, count + reach - block)
        window = jnp.concatenate(
            [
                rows[(block + tile - reach) * bins : (block + tile - reach + 1) * bins]
                for tile in range(low, high)
            ],
            axis=1,
        )
        total = jnp.dot(
            window,
            az_tiles[low:high].reshape((high - low) * WIDE, WIDE),
            preferred_element_type=jnp.float32,
        )
        for part in range(2):
            image[part, 0, :, block * BLK : (block + 1) * BLK] = total[
                :, part * BLK : (part + 1) * BLK
            ]
        done(block)


def column(image, out, sems, block):
    span = pl.ds(pl.multiple_of(block * BLK, BLK), BLK)
    return pltpu.make_async_copy(image.at[:, :, :, span], out.at[:, :, :, span], sems.at[block])


def azimuth_body(steps, az_tiles, *rest):
    *parts, out, rows, image, sems = rest
    bins = image.shape[2]
    count = image.shape[3] // BLK
    if steps:
        azimuth_rows(bins, steps, parts, rows)
    else:
        rows[...] = parts[0][...]
    azimuth_blocks(
        bins,
        count,
        rows,
        az_tiles,
        image,
        lambda block: column(image, out, sems, block).start(),
    )
    for block in range(count):
        column(image, out, sems, block).wait()


def azimuth(steps, count, az_tiles, parts):
    bins = sum(part.shape[0] for part in parts) // count
    shape = (2, 1, bins, count * BLK)
    return call(
        functools.partial(azimuth_body, steps),
        "azimuth",
        jax.ShapeDtypeStruct(shape, jnp.float32),
        [VMEM()] * (1 + len(parts)),
        HBM(),
        [
            pltpu.VMEM((count * bins, WIDE), jnp.bfloat16),
            pltpu.VMEM(shape, jnp.float32),
            pltpu.SemaphoreType.DMA((count,)),
        ],
    )(az_tiles, *parts)


def azimuth_most_body(steps, absent, az_tiles, *rest):
    *parts, image, rows = rest
    bins = image.shape[2]
    azimuth_rows(bins, [absent], [jnp.zeros((bins, WIDE), jnp.bfloat16)], rows)
    azimuth_rows(bins, steps, parts, rows)
    azimuth_blocks(bins, image.shape[3] // BLK, rows, az_tiles, image)


def azimuth_most(steps, absent, az_tiles, parts):
    bins = parts[0].shape[0]
    count = len(steps) + 1
    return call(
        functools.partial(azimuth_most_body, steps, absent),
        "azimuth_most",
        jax.ShapeDtypeStruct((2, 1, bins, count * BLK), jnp.float32),
        [VMEM()] * (1 + len(parts)),
        VMEM(),
        [pltpu.VMEM((count * bins, WIDE), jnp.bfloat16)],
    )(az_tiles, *parts)


def azimuth_last_body(step, az_tiles, most, part, out, image, sems):
    count = most.shape[3] // BLK
    low = (lax.axis_index("pulse") ^ step) - AZ_TILES // 2

    def move(source, place, block):
        span = pl.ds(pl.multiple_of(block * BLK, BLK), BLK)
        return pltpu.make_async_copy(
            source.at[:, :, :, pl.ds(pl.multiple_of(place * BLK, BLK), BLK)],
            out.at[:, :, :, span],
            sems.at[block],
        )

    for block in range(count):
        pl.when((block < low) | (block >= low + AZ_TILES))(move(most, block, block).start)
    for i in range(AZ_TILES):
        total = jnp.dot(
            part[...], az_tiles[AZ_TILES - 1 - i], preferred_element_type=jnp.float32
        )
        block = low + i
        held = pl.ds(pl.multiple_of(jnp.clip(block, 0, count - 1) * BLK, BLK), BLK)
        for side in range(2):
            image[side, 0, :, i * BLK : (i + 1) * BLK] = (
                most[side, 0, :, held] + total[:, side * BLK : (side + 1) * BLK]
            )
        inside = (block >= 0) & (block < count)
        pl.when(inside)(lambda i=i, block=block: move(image, i, block).start())
    for block in range(count):
        move(most, block, block).wait()


def azimuth_last(step, az_tiles, most, part):
    return call(
        functools.partial(azimuth_last_body, step),
        "azimuth_last",
        jax.ShapeDtypeStruct(most.shape, most.dtype),
        [VMEM()] * 3,
        HBM(),
        [
            pltpu.VMEM(most.shape[:3] + (AZ_TILES * BLK,), jnp.float32),
            pltpu.SemaphoreType.DMA((most.shape[3] // BLK,)),
        ],
    )(az_tiles, most, part)


def per_device(echoes, range_ref, band_weights, band_offsets, azimuth_ref):
    quarter_len = echoes.shape[2]
    peers = lax.axis_size("pulse")
    quarters = lax.axis_size("rng")
    bins = quarter_len // peers
    range_tiles = make_range_tiles(range_ref)
    near, down, up = pack(echoes, range_tiles)
    cores = [(i, i + 1) for i in range(0, quarters - 1, 2)]
    chips = [(i, i + 1) for i in range(1, quarters - 1, 2)]
    near = lax.ppermute(near, "rng", cores + [(j, i) for i, j in cores])
    down = lax.ppermute(down, "rng", [(j, i) for i, j in chips])
    up = lax.ppermute(up, "rng", chips)
    weights, offsets = band_weights, band_offsets.reshape(-1, BLK)
    samples = lay_out(echoes)

    if bins != GROUP or peers != 8:
        mine, az_tiles = whole_quarter(
            samples, near, down, up, range_tiles, weights, offsets, azimuth_ref
        )
        swapped = lax.all_to_all(
            mine.reshape(peers, bins, WIDE), "pulse", split_axis=0, concat_axis=0, tiled=True
        )
        return azimuth(None, peers, az_tiles, [swapped.reshape(mine.shape)])

    def send(piece, k):
        return lax.ppermute(piece, "pulse", [(i, i ^ k) for i in range(peers)])

    samples, made = first_range(
        [5, 4], samples, near, down, up, range_tiles, weights, offsets
    )
    ready = dict(zip([5, 4], made))
    for some in [[6, 7], [1], [2, 3]]:
        made = next_range([some], made[0], samples, range_tiles, weights, offsets)
        ready.update(zip(some, made))
    parts = {}
    parts[5] = send(ready[5], 5)
    parts[4] = send(ready[4], 4)
    parts[6] = send(ready[6], 6)
    parts[7] = send(ready[7], 7)
    parts[1] = send(ready[1], 1)
    parts[3] = send(gate([ready[3]], (parts[4],))[0], 3)
    parts[2] = send(gate([ready[2]], (parts[5],))[0], 2)
    after = parts[4]
    parts[0], az_tiles = own_range(after, samples, range_tiles, weights, offsets, azimuth_ref)
    parts.update(zip([6, 7], gate((parts[6], parts[7],), (), 1000000000)))
    parts.update(zip([6, 7, 1], gate((parts[6], parts[7], parts[1],), (), 200000000)))
    last = parts.pop(2)
    most = azimuth_most(list(parts), 2, az_tiles, list(parts.values()))
    return azimuth_last(2, az_tiles, most, last)


def solution(mesh):
    return jax.shard_map(
        per_device,
        mesh=mesh,
        in_specs=(P(None, "pulse", "rng"), P(), P(None, "rng"), P("rng"), P()),
        out_specs=P(None, "rng", "pulse", None),
        check_vma=False,
    )
```
